32 devices in a mesh: expert: 16 (over z, y, x), hsplit: 2 (over core).
Axes of the slice: x: 2, y: 2, z: 4, core: 2. Of those that a mesh axis runs over, the one named last changes fastest.
Arguments:
- tokens: bfloat16 [256, 7168], P('expert'), may hold values from -6 to 6
- routes: int32 [256, 8], P('expert'), may hold values from 0 to 15, all different within a row; in each aligned block of 16 rows (0 to 15, 16 to 31, ...) at most 16 rows name the same one
- route_weights: float32 [256, 8], P('expert'), may hold values from 0.05 to 0.6
- gate_weight: bfloat16 [16, 7168, 2048], P('expert', None, 'hsplit'), may hold values from -0.0625 to 0.0625
- up_weight: bfloat16 [16, 7168, 2048], P('expert', None, 'hsplit'), may hold values from -0.0625 to 0.0625
- down_weight: bfloat16 [16, 2048, 7168], P('expert', 'hsplit'), may hold values from -0.125 to 0.125
Outputs:
- routed_out: bfloat16 [256, 7168], P('expert', 'hsplit')
The draws below stay inside these ranges and needn't reach their ends.
Inputs may be any that keep to these rules, and one draw needn't show every extreme that they name: `routes`: each token names 8 different experts. In each aligned block of 16 tokens (one of 1 block of the tokens of one index of the expert axis) some expert is named by every token of the block.
All inputs are finite; a program needn't handle non-finite values.
Results may differ from the reference program's by a relative error of at most 0.02.
Values may be sent and summed in bfloat16 or wider, within the bound.
No kernel may reach another device: no remote copies, remote signals or barrier semaphores. Data moves between devices by JAX's collectives and lax.ppermute only.
A program may use at most 128 MiB of HBM per device.

```python
import math
import jax
import jax.numpy as jnp
import numpy as np
from jax import lax

D = 7168
FF = 2048
TOP = 8
EXPERTS = 16
GROUP = 1
MOST = 16
TOKENS = 256
N_EXPERT = 16
N_HSPLIT = 2


def level_of(rng, shape, shards, smallest, top_value):
    def one(axis_at, blocks):
        steps = jax.random.uniform(jax.random.fold_in(jax.random.fold_in(rng, 6), axis_at), (blocks,), jnp.float32, smallest / len(shards), top_value / len(shards))
        return jnp.repeat(jnp.exp(steps), shape[axis_at] // blocks).reshape((-1,) + (1,) * (len(shape) - axis_at - 1))

    level = one(*shards[0])
    for cut in shards[1:]:
        level = level * one(*cut)
    return level


def deal_out(key, own, number, rows, amount, top, limit, skew):
    order = jax.random.permutation(key, amount)
    heavy_load, usual = load_shares(amount, rows * top, limit, skew, True), load_shares(amount, rows * top, limit, skew, False)
    places = jnp.arange(amount)

    def named(sizes, rotation):
        used = int((sizes > 0).sum())
        fixed = max(1, used // 4)
        shifted = fixed + (places - fixed + rotation * (used - fixed)) % max(1, amount - fixed)
        return jnp.zeros((amount,), jnp.int32).at[order[jnp.where(places < fixed, places, shifted)]].set(jnp.asarray(sizes, jnp.int32))

    sizes = jnp.where(number % 4 == 0, named(heavy_load, number // 4), named(usual, number - number // 4 - 1))
    mixed = jax.random.permutation(jax.random.fold_in(own, 3), amount)
    donor, taker = mixed[0:amount // 2 * 2:2], mixed[1:amount // 2 * 2:2]
    slack = jnp.minimum(sizes[donor] - 1, limit - sizes[taker]) // 2
    slack = jnp.where((donor == order[0]) | (taker == order[0]) | (sizes[taker] == 0), 0, jnp.maximum(slack, 0))
    shifted = jax.random.randint(jax.random.fold_in(own, 4), (amount // 2,), 0, 1 << 20) % (slack + 1)
    sizes = sizes.at[donor].add(-shifted).at[taker].add(shifted)
    members = jnp.searchsorted(jnp.cumsum(sizes), jnp.arange(rows * top), side="right").astype(jnp.int32)
    grid = members.reshape(top, rows).T
    grid = grid[jax.random.permutation(jax.random.fold_in(own, 1), rows)]
    rotation = jax.random.randint(jax.random.fold_in(own, 2), (rows, 1), 0, top)
    return jnp.take_along_axis(grid, (jnp.arange(top)[None, :] + rotation) % top, axis=1)


def load_shares(amount, total, reach, skew, full):
    weights = [(1 << 20) // math.isqrt(standing ** skew) + 1 for standing in range(1, amount + 1)]
    largest = reach if full else min(reach, max(-(-total // amount), total * weights[0] // sum(weights)))
    least = 1 if total - largest >= amount - 1 else 0
    counts, spare = [largest] + [least] * (amount - 1), total - largest - least * (amount - 1)
    while spare > 0:
        free = [i for i in range(1, amount) if counts[i] < largest] or [i for i in range(1, amount) if counts[i] < reach]
        whole, remaining = sum([weights[i] for i in free]), spare
        for i in free:
            more = min(reach - counts[i], max(1, remaining * weights[i] // whole), spare)
            counts[i] = counts[i] + more
            spare = spare - more
    return np.array(counts)


def bell_draw(key, dims, width, bound, pieces=(), held_as=jnp.bfloat16):
    loudness = level_of(key, dims, pieces, -0.22, 0.18) if pieces else 1.0
    drawn = jax.random.normal(key, dims, jnp.float32) * width * loudness
    return jnp.minimum(jnp.maximum(drawn, -bound), bound).astype(held_as)


def setup_inputs(seed: int = 0) -> dict:
    seeds = jax.random.split(jax.random.key(seed), 7)
    tokens = bell_draw(seeds[0], (TOKENS, D), 1.0, 6.0, ((0, 16),))
    routes_keys = jax.random.split(jax.random.fold_in(seeds[1], 1), TOKENS // MOST)
    routes_turns = jax.random.permutation(jax.random.fold_in(seeds[1], 3), TOKENS // MOST)
    routes = jax.vmap(lambda own, number: deal_out(jax.random.fold_in(seeds[1], 2), own, number, MOST, EXPERTS, TOP, MOST, 2))(routes_keys, routes_turns).reshape((TOKENS, TOP))
    route_weights = jnp.clip(0.05 + 0.55 * jax.random.uniform(seeds[2], (TOKENS, TOP), jnp.float32) ** level_of(seeds[2], (TOKENS, TOP), ((0, 16),), -0.2, 0.2), 0.05, 0.6)
    gate_weight = bell_draw(seeds[3], (N_EXPERT, D // GROUP, FF), D ** -0.5, 0.0625, ((0, 16), (2, 2)))
    up_weight = bell_draw(seeds[4], (N_EXPERT, D // GROUP, FF), D ** -0.5, 0.0625, ((0, 16), (2, 2)))
    down_weight = bell_draw(seeds[5], (N_EXPERT, FF, D // GROUP), FF ** -0.5, 0.125, ((0, 16), (1, 2)))
    return dict(tokens=tokens, routes=routes, route_weights=route_weights, gate_weight=gate_weight, up_weight=up_weight, down_weight=down_weight)


def reference(tokens, routes, route_weights, gate_weight, up_weight, down_weight):
    model_width = tokens.shape[1]
    piece_width = model_width // (GROUP * N_HSPLIT)
    gate_all = gate_weight.reshape(EXPERTS, model_width, FF)
    up_all = up_weight.reshape(EXPERTS, model_width, FF)
    down_all = down_weight.reshape(EXPERTS, GROUP, FF, N_HSPLIT, piece_width).transpose(0, 2, 3, 1, 4).reshape(EXPERTS, FF, model_width)
    capacity = GROUP * N_EXPERT * MOST
    token_ids = jnp.broadcast_to(jnp.arange(TOKENS, dtype=jnp.int32)[:, None], (TOKENS, TOP)).reshape(-1)
    flat_routes = routes.reshape(-1)
    flat_weights = route_weights.reshape(-1)

    def one_expert(running, packed):
        expert_id, w_gate, w_up, w_down = packed
        hits = flat_routes == expert_id
        ranking = jnp.cumsum(hits.astype(jnp.int32)) - 1
        target = jnp.where(hits, ranking, capacity).astype(jnp.int32)
        chosen = jnp.zeros((capacity,), jnp.int32).at[target].set(token_ids, mode="drop")
        factor = jnp.zeros((capacity,), jnp.float32).at[target].set(flat_weights, mode="drop")
        picked = tokens[chosen]
        gate_value = jnp.dot(picked, w_gate, preferred_element_type=jnp.float32)
        up_value = jnp.dot(picked, w_up, preferred_element_type=jnp.float32)
        hidden = lax.optimization_barrier((jax.nn.silu(gate_value) * up_value).astype(jnp.bfloat16))
        shares = hidden.reshape(capacity, N_HSPLIT, FF // N_HSPLIT).transpose(1, 0, 2).astype(jnp.float32)
        down_parts = w_down.reshape(N_HSPLIT, FF // N_HSPLIT, model_width).astype(jnp.float32)
        partial_value = jnp.einsum("hcf,hfd->hcd", shares, down_parts)
        partial_value = lax.optimization_barrier(partial_value.astype(jnp.bfloat16))
        expert_out = jnp.sum(partial_value.astype(jnp.float32), axis=0)
        expert_out = lax.optimization_barrier(expert_out.astype(jnp.bfloat16))
        running = running.at[chosen].add(factor[:, None] * expert_out.astype(jnp.float32))
        return running, None

    start_value = jnp.zeros((TOKENS, model_width), jnp.float32)
    running, _ = lax.scan(one_expert, start_value, (jnp.arange(EXPERTS, dtype=jnp.int32), gate_all, up_all, down_all))
    return running.astype(jnp.bfloat16)
```

```python
import functools

import jax
import jax.numpy as jnp
from jax import lax
from jax.experimental import pallas as pl
from jax.experimental.pallas import tpu as pltpu
from jax.sharding import PartitionSpec as P

EXPERTS = 16
LANES = 128
INNER = 4


def inner_route(count, apart):
    return [(i, i ^ apart) for i in range(count)]


def outer_route(count, apart):
    return [(i, i ^ (INNER * apart)) for i in range(count)]


def send(block, route):
    return lax.ppermute(block, "expert", route)


def other_core(block):
    return lax.ppermute(block, "hsplit", [(0, 1), (1, 0)])


def spread(block, routes):
    return [block] + [send(block, route) for route in routes]


def assemble(x_ref, a_refs, b_refs, rows, first):
    for kp in range(INNER):
        x_ref[kp * INNER * rows : (kp + 1) * INNER * rows, :first] = a_refs[kp][...]
        for kz in range(INNER):
            at = (kp * INNER + kz) * rows
            x_ref[at : at + rows, first:] = b_refs[kz][
                kp * rows : (kp + 1) * rows, : x_ref.shape[1] - first
            ]


def own_kernel(rows, first, where, *refs):
    a_refs, b_refs = refs[:INNER], refs[INNER : 2 * INNER]
    wg_ref, wu_ref, gate_ref, up_ref, x_ref = refs[2 * INNER :]

    @pl.when(pl.program_id(0) == 0)
    def _():
        assemble(x_ref, a_refs, b_refs, rows, first)

    gate_ref[...] = jnp.dot(x_ref[...], wg_ref[0], preferred_element_type=jnp.float32)
    up_ref[...] = jnp.dot(x_ref[...], wu_ref[0], preferred_element_type=jnp.float32)


def rest_kernel(rows, first, second, where, *refs):
    a_refs, b_refs = refs[:INNER], refs[INNER : 2 * INNER]
    wg_ref, wu_ref, gate_ref, up_ref, hid_ref, x_ref, scale_ref = refs[2 * INNER :]

    @pl.when(pl.program_id(0) == 0)
    def _():
        assemble(x_ref, a_refs, b_refs, rows, first)
        expert = where[1]
        lane = lax.broadcasted_iota(jnp.int32, (rows, LANES), 1)
        mine = (lane == expert) | (lane == expert + EXPERTS)
        for kp in range(INNER):
            for kz in range(INNER):
                at = (kp * INNER + kz) * rows
                extra = b_refs[kz][kp * rows : (kp + 1) * rows, second:].astype(jnp.float32)
                total = jnp.sum(jnp.where(mine, extra, 0.0), axis=1, keepdims=True)
                scale_ref[at : at + rows, :] = jnp.broadcast_to(total, (rows, LANES))

    gate = gate_ref[...] + jnp.dot(x_ref[...], wg_ref[0], preferred_element_type=jnp.float32)
    up = up_ref[...] + jnp.dot(x_ref[...], wu_ref[0], preferred_element_type=jnp.float32)
    hidden = gate / (1.0 + jnp.exp(-gate)) * up * scale_ref[:, :1]
    hid_ref[...] = hidden.astype(hid_ref.dtype)


def down_kernel(where, hid_ref, w_ref, out_ref):
    out_ref[...] = jnp.dot(hid_ref[...], w_ref[...], preferred_element_type=jnp.float32).astype(
        out_ref.dtype
    )


def down_inner_kernel(rows, where, hid_ref, w_ref, far_ref, *out_refs):
    total = jnp.dot(hid_ref[...], w_ref[...], preferred_element_type=jnp.float32)
    total = (total + far_ref[...].astype(jnp.float32)).astype(jnp.bfloat16)
    span = INNER * rows
    for kp in range(INNER):
        out_refs[kp][...] = total[kp * span : (kp + 1) * span]


def down_outer_kernel(rows, where, hid_ref, w_ref, far_ref, *out_refs):
    total = jnp.dot(hid_ref[...], w_ref[...], preferred_element_type=jnp.float32)
    total = (total + far_ref[...].astype(jnp.float32)).astype(jnp.bfloat16)
    for kz in range(INNER):
        for kp in range(INNER):
            at = (kp * INNER + kz) * rows
            out_refs[kz][kp * rows : (kp + 1) * rows, :] = total[at : at + rows]


def sum_split_kernel(rows, *refs):
    total = functools.reduce(
        jnp.add, [ref[...].astype(jnp.float32) for ref in refs[:INNER]]
    ).astype(jnp.bfloat16)
    for k in range(INNER):
        refs[INNER + k][...] = total[k * rows : (k + 1) * rows]


def sum_join_kernel(first, *refs):
    out_ref = refs[-1]
    for at, part in ((0, refs[:INNER]), (first, refs[INNER : 2 * INNER])):
        total = functools.reduce(jnp.add, [ref[...].astype(jnp.float32) for ref in part])
        out_ref[:, at : at + total.shape[1]] = total.astype(out_ref.dtype)


def params(mib):
    return pltpu.CompilerParams(vmem_limit_bytes=mib << 20)


def up_call(kernel, where, pieces, gate_weight, up_weight, far, sums, out_shapes, scratch, name):
    half = gate_weight.shape[0] // 2
    units = gate_weight.shape[1]
    tile = min(256, units)
    tokens = INNER * pieces[0].shape[0]
    whole = [pl.BlockSpec(p.shape, lambda n, w: (0, 0)) for p in pieces]
    weight = pl.BlockSpec(
        (1, half, tile), (lambda n, w: (1 - w[0], 0, n)) if far else (lambda n, w: (w[0], 0, n))
    )
    columns = pl.BlockSpec((tokens, tile), lambda n, w: (0, n))
    flops = 2 * 2 * tokens * half * units
    return pl.pallas_call(
        kernel,
        out_shape=out_shapes,
        grid_spec=pltpu.PrefetchScalarGridSpec(
            num_scalar_prefetch=1,
            grid=(units // tile,),
            in_specs=whole + [weight, weight] + [columns] * len(sums),
            out_specs=[columns] * len(out_shapes),
            scratch_shapes=scratch,
        ),
        compiler_params=params(32),
        cost_estimate=pl.CostEstimate(
            flops=flops, bytes_accessed=4 * half * units, transcendentals=0
        ),
        name=name,
    )(
        where,
        *pieces,
        gate_weight.reshape(2, half, units),
        up_weight.reshape(2, half, units),
        *sums,
    )


def down_call(kernel, where, hidden, weight, far, start, width, tile, received, out_shapes, name):
    tokens, units = hidden.shape
    per_half = weight.shape[1] // 2 // tile
    base = start // tile
    if far:
        pick = lambda n, w: (0, (1 - w[0]) * per_half + base + n)
    else:
        pick = lambda n, w: (0, w[0] * per_half + base + n)
    extra = [pl.BlockSpec((tokens, tile), lambda n, w: (0, n))] * len(received)
    return pl.pallas_call(
        kernel,
        out_shape=out_shapes,
        grid_spec=pltpu.PrefetchScalarGridSpec(
            num_scalar_prefetch=1,
            grid=(width // tile,),
            in_specs=[
                pl.BlockSpec((tokens, units), lambda n, w: (0, 0)),
                pl.BlockSpec((units, tile), pick),
            ]
            + extra,
            out_specs=[pl.BlockSpec((s.shape[0], tile), lambda n, w: (0, n)) for s in out_shapes],
        ),
        compiler_params=params(24),
        cost_estimate=pl.CostEstimate(
            flops=2 * tokens * units * width, bytes_accessed=2 * units * width, transcendentals=0
        ),
        name=name,
    )(where, hidden, weight, *received)


def local_single(tokens, routes, route_weights, gate_weight, up_weight, down_weight):
    rows, width = tokens.shape
    owners = lax.axis_size("expert")
    units = gate_weight.shape[2]
    half = width // 2
    tile = 512
    first = half * 5 // 7 // tile * tile
    second = half - first
    total_rows = owners * rows
    core = lax.axis_index("hsplit")
    where = jnp.stack([core, lax.axis_index("expert")]).astype(jnp.int32)
    gate_weight, up_weight, down_weight = gate_weight[0], up_weight[0], down_weight[0]
    by_inner = [inner_route(owners, k) for k in range(1, INNER)]
    by_outer = [outer_route(owners, k) for k in range(1, INNER)]

    named = routes[:, :, None] == jnp.arange(EXPERTS, dtype=jnp.int32)[None, None, :]
    table = jnp.sum(jnp.where(named, route_weights[:, :, None], 0.0), axis=1)
    high = table.astype(jnp.bfloat16)
    low = (table - high.astype(jnp.float32)).astype(jnp.bfloat16)
    extra = jnp.pad(jnp.concatenate([high, low], axis=1), ((0, 0), (0, LANES - 2 * EXPERTS)))

    mine = lax.dynamic_slice_in_dim(tokens, core * half, half, 1)
    a_block = mine[:, :first]
    b_block = jnp.concatenate([mine[:, first:], extra], axis=1)

    z_blocks = spread(a_block, by_outer)
    p_blocks = spread(b_block, by_inner)
    a_pieces = spread(jnp.concatenate(z_blocks, axis=0), by_inner)
    b_pieces = spread(jnp.concatenate(p_blocks, axis=0), by_outer)
    pieces = a_pieces + b_pieces
    far_pieces = [other_core(p) for p in pieces]

    f32 = functools.partial(jax.ShapeDtypeStruct, dtype=jnp.float32)
    b16 = functools.partial(jax.ShapeDtypeStruct, dtype=jnp.bfloat16)
    x_scratch = pltpu.VMEM((total_rows, half), jnp.bfloat16)
    sums = up_call(
        functools.partial(own_kernel, rows, first),
        where,
        pieces,
        gate_weight,
        up_weight,
        False,
        [],
        [f32((total_rows, units))] * 2,
        [x_scratch],
        "own_columns",
    )
    (hidden,) = up_call(
        functools.partial(rest_kernel, rows, first, second),
        where,
        far_pieces,
        gate_weight,
        up_weight,
        True,
        sums,
        [b16((total_rows, units))],
        [x_scratch, pltpu.VMEM((total_rows, LANES), jnp.float32)],
        "other_columns",
    )

    def partial_out(start, span, name):
        (out,) = down_call(
            down_kernel, where, hidden, down_weight, True, start, span, tile, [],
            [b16((total_rows, span))], name,
        )
        return other_core(out)

    def summed_out(kernel, start, span, received, name):
        return down_call(
            functools.partial(kernel, rows), where, hidden, down_weight, False, start, span, tile,
            [received], [b16((INNER * rows, span))] * INNER, name,
        )

    b_far = partial_out(first, second, "down_far_b")
    a_far = partial_out(0, first, "down_far_a")
    b_out = summed_out(down_outer_kernel, first, second, b_far, "down_own_b")
    a_out = summed_out(down_inner_kernel, 0, first, a_far, "down_own_a")

    def back(parts, routes_out):
        return [parts[0]] + [send(p, r) for p, r in zip(parts[1:], routes_out)]

    def sum_split(parts, span, name):
        return pl.pallas_call(
            functools.partial(sum_split_kernel, rows),
            out_shape=[b16((rows, span))] * INNER,
            compiler_params=params(16),
            name=name,
        )(*parts)

    b_mid = sum_split(back(b_out, by_outer), second, "sum_b")
    a_mid = sum_split(back(a_out, by_inner), first, "sum_a")
    b_end = back(b_mid, by_inner)
    a_end = back(a_mid, by_outer)
    return pl.pallas_call(
        functools.partial(sum_join_kernel, first),
        out_shape=b16((rows, half)),
        compiler_params=params(16),
        name="sum_out",
    )(*a_end, *b_end)


def as_sent(array):

    def short(part):
        return part.astype(jnp.bfloat16) if part.dtype == jnp.float32 else part

    return jax.tree.map(short, array)


def swapped(block, axis, apart):
    count = lax.axis_size(axis)
    route = []
    for low in range(count):
        high = low | 1 << apart
        if high != low and high < count:
            route += [(low, high), (high, low)]
    return lax.ppermute(block, axis, route)


def expert_rows(tok_rows, full_gate, full_up, full_down):
    gate_value = jnp.dot(tok_rows, full_gate, preferred_element_type=jnp.float32)
    up_value = jnp.dot(tok_rows, full_up, preferred_element_type=jnp.float32)
    hidden = (jax.nn.silu(gate_value) * up_value).astype(jnp.bfloat16)
    partial_value = jnp.dot(hidden, full_down, preferred_element_type=jnp.float32)
    return lax.optimization_barrier(partial_value.astype(jnp.bfloat16))


def local_grouped(tokens, routes, route_weights, gate_weight, up_weight, down_weight):
    tok_dev, model_width = tokens.shape
    top_k = routes.shape[1]
    owners = lax.axis_size("expert")
    splits = lax.axis_size("hsplit")
    group_size = owners // EXPERTS
    group_bits = group_size.bit_length() - 1
    most = tok_dev // group_size
    slot_count = owners * most
    slice_width = model_width // group_size
    piece_width = slice_width // splits
    position = lax.axis_index("expert")
    token_group = lax.broadcasted_iota(jnp.int32, (tok_dev, top_k), 0) // most
    owner_of = (group_size * routes + token_group).reshape(-1)
    owner_hit = (owner_of[:, None] == jnp.arange(owners, dtype=jnp.int32)[None, :]).astype(
        jnp.int32
    )
    earlier = jnp.cumsum(owner_hit, axis=0) - owner_hit
    ranking = jnp.sum(earlier * owner_hit, axis=1)
    slot_of = owner_of * most + ranking
    slot_grid = slot_of.reshape(tok_dev, top_k)
    selector = jnp.any(
        slot_grid[:, :, None] == jnp.arange(slot_count, dtype=jnp.int32)[None, None, :], axis=1
    ).astype(jnp.bfloat16)
    outgoing = jnp.einsum("ts,td->sd", selector, tokens, preferred_element_type=jnp.float32).astype(
        jnp.bfloat16
    )
    outgoing = outgoing.reshape(owners, most, model_width)
    stacked = (gate_weight, up_weight, down_weight)
    for level in range(group_bits):
        partner = jax.tree.map(
            lambda part, own: part.astype(own.dtype),
            swapped(as_sent(stacked), "expert", level),
            stacked,
        )
        upper = position >> level & 1 == 1
        stacked = tuple(
            (
                jnp.where(
                    upper,
                    jnp.concatenate([far_piece, near_piece], axis=0),
                    jnp.concatenate([near_piece, far_piece], axis=0),
                )
                for near_piece, far_piece in zip(stacked, partner)
            )
        )
    share_units = gate_weight.shape[2]
    full_gate = stacked[0].reshape(model_width, share_units)
    full_up = stacked[1].reshape(model_width, share_units)
    full_down = stacked[2].transpose(1, 0, 2).reshape(share_units, group_size, splits, piece_width)
    full_down = full_down.transpose(0, 2, 1, 3).reshape(share_units, model_width)
    arrived = lax.all_to_all(outgoing, "expert", split_axis=0, concat_axis=0, tiled=True)
    flat_rows = arrived.reshape(-1, model_width)
    partials = expert_rows(flat_rows, full_gate, full_up, full_down).reshape(arrived.shape)
    partials = partials.reshape(slot_count, model_width)
    summed = lax.psum_scatter(
        partials.astype(jnp.float32).astype(jnp.bfloat16), "hsplit", scatter_dimension=1, tiled=True
    )
    results = summed.reshape(owners, most, -1)
    returned = lax.all_to_all(results, "expert", split_axis=0, concat_axis=0, tiled=True)
    picked = returned.reshape(slot_count, -1)[slot_of].astype(jnp.float32)
    weighted = picked.reshape(tok_dev, top_k, -1) * route_weights[:, :, None]
    return jnp.sum(weighted, axis=1).astype(jnp.bfloat16)


def solution(mesh):
    placed = (
        P("expert", None),
        P("expert", None),
        P("expert", None),
        P("expert", None, "hsplit"),
        P("expert", None, "hsplit"),
        P("expert", "hsplit", None),
    )
    single = mesh.shape["expert"] == EXPERTS and mesh.shape["hsplit"] == 2
    return jax.shard_map(
        local_single if single else local_grouped,
        mesh=mesh,
        in_specs=placed,
        out_specs=P("expert", "hsplit"),
        check_vma=False,
    )
```

```python
import functools

import jax
import jax.numpy as jnp
from jax import lax
from jax.experimental import pallas as pl
from jax.experimental.pallas import tpu as pltpu
from jax.sharding import PartitionSpec as P

EXPERTS = 16
LANES = 128
INNER = 4


def exchanged(array, even, odd):
    owners = lax.axis_size("expert")
    route = []
    for core, apart in enumerate((even, odd)):
        route += [(2 * i + core, 2 * (i ^ apart) + core) for i in range(owners)]
    return lax.ppermute(array, ("expert", "hsplit"), route)


def first_hop(array, k):
    return exchanged(array, INNER * k, k)


def second_hop(array, k):
    return exchanged(array, k, INNER * k)


def other_core(array):
    return lax.ppermute(array, "hsplit", [(0, 1), (1, 0)])


VMEM = pl.BlockSpec(memory_space=pltpu.VMEM)
HBM = pl.BlockSpec(memory_space=pltpu.HBM)
TILE = 256


def kept(rows, columns, dtype=jnp.bfloat16):
    return pltpu.VMEM((rows, columns), dtype)


def call(kernel, out_shape, args, name, flops=0, moved=0, specs=None, scratch=(), mib=4):
    return pl.pallas_call(
        kernel,
        out_shape=out_shape,
        in_specs=specs or [VMEM] * len(args),
        out_specs=jax.tree.map(lambda _: VMEM, out_shape),
        scratch_shapes=scratch,
        compiler_params=pltpu.CompilerParams(vmem_limit_bytes=mib << 20),
        cost_estimate=pl.CostEstimate(flops=flops, bytes_accessed=moved, transcendentals=0),
        name=name,
    )(*args)


def fetches(wanted):
    args = [pltpu.with_memory_space_constraint(w[0], pltpu.HBM) for w in wanted]
    specs = [HBM] * len(wanted)
    outs = []
    for weight, axis, _, _, span in wanted:
        shape = list(weight.shape)
        shape[axis] = span
        outs.append(kept(*shape))

    def copies(in_refs, out_refs, sems):
        found = []
        for n, (weight, axis, own, start, span) in enumerate(wanted):
            core = lax.axis_index("hsplit")
            core_at = core if own else 1 - core
            at = pl.multiple_of(core_at * (weight.shape[axis] // 2) + start, LANES)
            ref = in_refs[n]
            part = ref.at[:, pl.ds(at, span)] if axis else ref.at[pl.ds(at, span)]
            found.append(pltpu.make_async_copy(part, out_refs[n], sems.at[n]))
        return found

    scratch = [pltpu.SemaphoreType.DMA((len(wanted),))] if wanted else []
    moved = sum(2 * 2 * o.shape[0] * o.shape[1] for o in outs)
    return args, specs, outs, scratch, moved, copies


def fetch(wanted, name):
    args, specs, outs, scratch, moved, copies = fetches(wanted)

    def kernel(*refs):
        found = copies(refs[: len(args)], refs[len(args) : -2], refs[-1])
        for copy in found:
            copy.start()
        refs[-2][...] = jnp.zeros(refs[-2].shape, refs[-2].dtype)
        for copy in found:
            copy.wait()

    results = call(
        kernel, outs + [kept(8, LANES, jnp.float32)], args, name, moved=moved,
        specs=specs, scratch=scratch, mib=2,
    )
    return results[:-1], results[-1]


def beside(copies, compute):
    for copy in copies:
        copy.start()
    if copies:
        pl.when(lax.axis_index("hsplit") >= 0)(compute)
    else:
        compute()
    for copy in copies:
        copy.wait()


def first_piece(tokens, routes, route_weights):
    rows, width = tokens.shape
    half = width // 2

    def kernel(tok_ref, routes_ref, weights_ref, out_ref):
        at = pl.multiple_of(lax.axis_index("hsplit") * half, LANES)
        out_ref[:, :half] = tok_ref[:, pl.ds(at, half)]
        expert = lax.broadcasted_iota(jnp.int32, (EXPERTS, rows), 0)
        table = jnp.zeros((EXPERTS, rows), jnp.float32)
        for k in range(routes_ref.shape[0]):
            named = routes_ref[k : k + 1, :] == expert
            table += jnp.where(named, weights_ref[k : k + 1, :], 0.0)
        high = table.astype(jnp.bfloat16)
        low = (table - high.astype(jnp.float32)).astype(jnp.bfloat16)
        both = jnp.concatenate([high, low], axis=0)
        shape = (2 * EXPERTS, LANES)
        lane = lax.broadcasted_iota(jnp.int32, shape, 1)
        place = (lax.broadcasted_iota(jnp.int32, shape, 0) == lane).astype(jnp.bfloat16)
        out_ref[:, half:] = lax.dot_general(
            both, place, (((0,), (0,)), ((), ())), preferred_element_type=jnp.float32
        ).astype(out_ref.dtype)

    return call(
        kernel, kept(rows, half + LANES), (tokens, routes.T, route_weights.T), "first_piece"
    )


def joined(parts, done, name):
    rows, width = parts[0].shape

    def kernel(*refs):
        for k in range(len(parts)):
            refs[-1][k * rows : (k + 1) * rows] = refs[k][...]

    return call(kernel, kept(len(parts) * rows, width), (*parts, done), name)


def up_own(pieces, weights, wanted, name):
    units = weights[0].shape[1]
    depth = weights[0].shape[0]
    rows = sum(p.shape[0] for p in pieces)
    more, more_specs, fetched, scratch, moved, copies = fetches(wanted)
    fixed = list(pieces) + list(weights)
    args = fixed + more
    shapes = [kept(rows, units, jnp.float32) for _ in range(2)]

    def kernel(*refs):
        outs = refs[len(args) : len(args) + 2]
        found = []
        if wanted:
            found = copies(refs[len(fixed) : len(args)], refs[len(args) + 2 : -1], refs[-1])

        def compute():
            for n in range(units // TILE):
                columns = slice(n * TILE, (n + 1) * TILE)
                x = jnp.concatenate([refs[p][:, :depth] for p in range(len(pieces))], axis=0)
                for which in range(2):
                    outs[which][:, columns] = jnp.dot(
                        x, refs[len(pieces) + which][:, columns], preferred_element_type=jnp.float32
                    )

        beside(found, compute)

    results = call(
        kernel, shapes + fetched, args, name, flops=4 * rows * units * depth, moved=moved,
        specs=[VMEM] * len(fixed) + more_specs, scratch=scratch, mib=8,
    )
    return results[:2], results[2:]


def hidden_call(pieces, last, weights, own_sums, far_sums, extras, wanted):
    units = weights[0].shape[1]
    depth = weights[0].shape[0]
    rows = pieces[0].shape[0]
    block_rows = rows // INNER
    more, more_specs, fetched, scratch, moved, copies = fetches(wanted)
    fixed = list(pieces) + list(weights)
    sums_at = len(fixed)
    for _, gate, up in own_sums + far_sums:
        fixed += [gate, up]
    extras_at = len(fixed)
    fixed += list(extras)
    args = fixed + more
    out_shape = kept(INNER * rows, units)

    def kernel(*refs):
        out_ref = refs[len(args)]
        scale_ref = refs[-1]
        found = copies(refs[len(fixed) : len(args)], refs[len(args) + 1 : -2], refs[-2])
        def compute():
            extra = jnp.concatenate(
                [refs[extras_at + k][:, depth:] for k in range(INNER)], axis=0
            ).astype(jnp.float32)
            lane = lax.broadcasted_iota(jnp.int32, extra.shape, 1)
            expert = lax.axis_index("expert")
            mine = (lane == expert) | (lane == expert + EXPERTS)
            total = jnp.sum(jnp.where(mine, extra, 0.0), axis=1, keepdims=True)
            scale_ref[...] = jnp.broadcast_to(total, scale_ref.shape)

            for n in range(units // TILE):
                columns = slice(n * TILE, (n + 1) * TILE)
                x = jnp.concatenate([refs[p][:, :depth] for p in range(len(pieces))], axis=0)
                both = []
                for which in range(2):
                    product = jnp.dot(
                        x, refs[len(pieces) + which][:, columns], preferred_element_type=jnp.float32
                    )
                    own, far = {}, {}
                    for n_sum, (held, _, _) in enumerate(own_sums):
                        for at, k in enumerate(held):
                            own[k] = (refs[sums_at + 2 * n_sum + which], at)
                    for n_sum, (held, _, _) in enumerate(far_sums):
                        for at, k in enumerate(held):
                            far[k] = (refs[sums_at + 2 * (len(own_sums) + n_sum) + which], at)
                    parts = []
                    for jj in range(INNER):
                        for ii in range(INNER):
                            ref, at = own[jj]
                            at = at * rows + ii * block_rows
                            mine_part = ref[at : at + block_rows, columns]
                            if ii in far:
                                ref, at = far[ii]
                                at = at * rows + jj * block_rows
                                other = ref[at : at + block_rows, columns]
                            else:
                                at = last.index(ii) * rows + jj * block_rows
                                other = product[at : at + block_rows]
                            parts.append(mine_part + other)
                    both.append(jnp.concatenate(parts, axis=0))
                gate, up = both
                scale = jnp.concatenate([scale_ref[...]] * (TILE // LANES), axis=1)
                hidden = gate / (1.0 + jnp.exp(-gate)) * up * scale
                out_ref[:, columns] = hidden.astype(out_ref.dtype)

        beside(found, compute)

    results = call(
        kernel, [out_shape] + fetched, args, "hidden",
        flops=4 * len(pieces) * rows * units * depth, moved=moved,
        specs=[VMEM] * len(fixed) + more_specs,
        scratch=scratch + [pltpu.VMEM((INNER * rows, LANES), jnp.float32)], mib=8,
    )
    return results[0], results[1:]


def down_far(hidden, weight, held, name, before=()):
    tokens, units = hidden.shape
    rows = tokens // INNER
    block_rows = rows // INNER
    span = weight.shape[1]

    def kernel(hid_ref, w_ref, *rest):
        out_ref = rest[-1]
        at = [jj * rows + k * block_rows for k in held for jj in range(INNER)]
        x = jnp.concatenate([hid_ref[a : a + block_rows] for a in at], axis=0)
        for at in range(0, span, TILE):
            out_ref[:, at : at + TILE] = jnp.dot(
                x, w_ref[:, at : at + TILE], preferred_element_type=jnp.float32
            ).astype(out_ref.dtype)

    out_rows = len(held) * rows
    return call(
        kernel, kept(out_rows, span), (hidden, weight, *before), name, flops=2 * out_rows * units * span
    )


def down_own(hidden, weight, received, held, name, before=()):
    tokens, units = hidden.shape
    rows = tokens // INNER
    span = weight.shape[1]

    def kernel(hid_ref, w_ref, far_ref, *rest):
        out_refs = rest[len(before) :]
        x = jnp.concatenate([hid_ref[k * rows : (k + 1) * rows] for k in held], axis=0)
        for at in range(0, span, TILE):
            columns = slice(at, at + TILE)
            total = jnp.dot(x, w_ref[:, columns], preferred_element_type=jnp.float32)
            total = (total + far_ref[:, columns].astype(jnp.float32)).astype(jnp.bfloat16)
            for n in range(len(held)):
                out_refs[n][:, columns] = total[n * rows : (n + 1) * rows]

    return call(
        kernel,
        [kept(rows, span) for _ in held],
        (hidden, weight, received, *before),
        name,
        flops=2 * len(held) * rows * units * span,
    )


def summed(refs):
    return functools.reduce(jnp.add, [ref[...].astype(jnp.float32) for ref in refs]).astype(
        jnp.bfloat16
    )


def sum_split(parts, name):
    rows, span = parts[0].shape
    rows //= INNER

    def kernel(*refs):
        total = summed(refs[:INNER])
        for k in range(INNER):
            refs[INNER + k][...] = total[k * rows : (k + 1) * rows]

    return call(kernel, [kept(rows, span) for _ in range(INNER)], parts, name)


def sum_out(parts):
    def kernel(*refs):
        refs[INNER][...] = summed(refs[:INNER])

    return call(kernel, jax.ShapeDtypeStruct(parts[0].shape, jnp.bfloat16), parts, "sum_out")


def local_single(tokens, routes, route_weights, gate_weight, up_weight, down_weight):
    rows, width = tokens.shape
    half = width // 2
    gate_weight, up_weight, down_weight = gate_weight[0], up_weight[0], down_weight[0]
    first = first_piece(tokens, routes, route_weights)

    def wanted(mine_too):
        return [(weight, 0, mine_too, 0, half) for weight in (gate_weight, up_weight)]

    firsts = {0: first}
    for k in (3, 2, 1):
        firsts[k] = first_hop(first, k)
    own_weights, done = fetch(wanted(True), "fetch_own")
    second = joined([firsts[k] for k in range(INNER)], done, "second")
    pieces = {0: second}
    for k in (3, 2, 1):
        pieces[k] = second_hop(second, k)
    far = {k: other_core(pieces[k]) for k in (0, 3, 2, 1)}

    far_weights, _ = fetch(wanted(False), "fetch_far")
    early, late = (0, 3), (2, 1)
    own_early, _ = up_own([pieces[k] for k in early], own_weights, [], "up_own_early")
    far_early, _ = up_own([far[k] for k in early], far_weights, [], "up_far_early")
    own_late, (down_other,) = up_own(
        [pieces[k] for k in late], own_weights, [(down_weight, 1, False, 0, half)],
        "up_own_late",
    )
    hidden, (down_mine,) = hidden_call(
        [far[k] for k in late],
        late,
        far_weights,
        [(early, *own_early), (late, *own_late)],
        [(early, *far_early)],
        [pieces[k] for k in range(INNER)],
        [(down_weight, 1, True, 0, half)],
    )

    middle, received, before = {}, {}, ()
    halves = (((3, 2), "a"), ((1, 0), "b"))
    for held, name in halves:
        sums = down_far(hidden, down_other, held, "down_far_" + name, before)
        received[held] = other_core(sums)
        before = (sums,)
    before = ()
    for held, name in halves:
        sums = down_own(hidden, down_mine, received[held], held, "down_own_" + name, before)
        before = (sums[0],)
        for k, part in zip(held, sums):
            middle[k] = second_hop(part, k) if k else part
    split = sum_split([middle[k] for k in range(INNER)], "sum_split")
    ended = [split[0]] + [first_hop(split[k], k) for k in (3, 2, 1)]
    return sum_out(ended)


def as_sent(array):

    def short(part):
        return part.astype(jnp.bfloat16) if part.dtype == jnp.float32 else part

    return jax.tree.map(short, array)


def swapped(block, axis, apart):
    count = lax.axis_size(axis)
    route = []
    for low in range(count):
        high = low | 1 << apart
        if high != low and high < count:
            route += [(low, high), (high, low)]
    return lax.ppermute(block, axis, route)


def expert_rows(tok_rows, full_gate, full_up, full_down):
    gate_value = jnp.dot(tok_rows, full_gate, preferred_element_type=jnp.float32)
    up_value = jnp.dot(tok_rows, full_up, preferred_element_type=jnp.float32)
    hidden = (jax.nn.silu(gate_value) * up_value).astype(jnp.bfloat16)
    partial_value = jnp.dot(hidden, full_down, preferred_element_type=jnp.float32)
    return lax.optimization_barrier(partial_value.astype(jnp.bfloat16))


def local_grouped(tokens, routes, route_weights, gate_weight, up_weight, down_weight):
    tok_dev, model_width = tokens.shape
    top_k = routes.shape[1]
    owners = lax.axis_size("expert")
    splits = lax.axis_size("hsplit")
    group_size = owners // EXPERTS
    group_bits = group_size.bit_length() - 1
    most = tok_dev // group_size
    slot_count = owners * most
    slice_width = model_width // group_size
    piece_width = slice_width // splits
    position = lax.axis_index("expert")
    token_group = lax.broadcasted_iota(jnp.int32, (tok_dev, top_k), 0) // most
    owner_of = (group_size * routes + token_group).reshape(-1)
    owner_hit = (owner_of[:, None] == jnp.arange(owners, dtype=jnp.int32)[None, :]).astype(
        jnp.int32
    )
    earlier = jnp.cumsum(owner_hit, axis=0) - owner_hit
    ranking = jnp.sum(earlier * owner_hit, axis=1)
    slot_of = owner_of * most + ranking
    slot_grid = slot_of.reshape(tok_dev, top_k)
    selector = jnp.any(
        slot_grid[:, :, None] == jnp.arange(slot_count, dtype=jnp.int32)[None, None, :], axis=1
    ).astype(jnp.bfloat16)
    outgoing = jnp.einsum("ts,td->sd", selector, tokens, preferred_element_type=jnp.float32).astype(
        jnp.bfloat16
    )
    outgoing = outgoing.reshape(owners, most, model_width)
    stacked = (gate_weight, up_weight, down_weight)
    for level in range(group_bits):
        partner = jax.tree.map(
            lambda part, own: part.astype(own.dtype),
            swapped(as_sent(stacked), "expert", level),
            stacked,
        )
        upper = position >> level & 1 == 1
        stacked = tuple(
            (
                jnp.where(
                    upper,
                    jnp.concatenate([far_piece, near_piece], axis=0),
                    jnp.concatenate([near_piece, far_piece], axis=0),
                )
                for near_piece, far_piece in zip(stacked, partner)
            )
        )
    share_units = gate_weight.shape[2]
    full_gate = stacked[0].reshape(model_width, share_units)
    full_up = stacked[1].reshape(model_width, share_units)
    full_down = stacked[2].transpose(1, 0, 2).reshape(share_units, group_size, splits, piece_width)
    full_down = full_down.transpose(0, 2, 1, 3).reshape(share_units, model_width)
    arrived = lax.all_to_all(outgoing, "expert", split_axis=0, concat_axis=0, tiled=True)
    flat_rows = arrived.reshape(-1, model_width)
    partials = expert_rows(flat_rows, full_gate, full_up, full_down).reshape(arrived.shape)
    partials = partials.reshape(slot_count, model_width)
    summed = lax.psum_scatter(
        partials.astype(jnp.float32).astype(jnp.bfloat16), "hsplit", scatter_dimension=1, tiled=True
    )
    results = summed.reshape(owners, most, -1)
    returned = lax.all_to_all(results, "expert", split_axis=0, concat_axis=0, tiled=True)
    picked = returned.reshape(slot_count, -1)[slot_of].astype(jnp.float32)
    weighted = picked.reshape(tok_dev, top_k, -1) * route_weights[:, :, None]
    return jnp.sum(weighted, axis=1).astype(jnp.bfloat16)


def solution(mesh):
    placed = (
        P("expert", None),
        P("expert", None),
        P("expert", None),
        P("expert", None, "hsplit"),
        P("expert", None, "hsplit"),
        P("expert", "hsplit", None),
    )
    single = mesh.shape["expert"] == EXPERTS and mesh.shape["hsplit"] == 2
    return jax.shard_map(
        local_single if single else local_grouped,
        mesh=mesh,
        in_specs=placed,
        out_specs=P("expert", "hsplit"),
        check_vma=False,
    )
```

```python
import functools

import jax
import jax.numpy as jnp
from jax import lax
from jax.experimental import pallas as pl
from jax.experimental.pallas import tpu as pltpu
from jax.sharding import PartitionSpec as P

EXPERTS = 16
LANES = 128
INNER = 4


def exchanged(array, even, odd):
    owners = lax.axis_size("expert")
    route = []
    for core, apart in enumerate((even, odd)):
        route += [(2 * i + core, 2 * (i ^ apart) + core) for i in range(owners)]
    return lax.ppermute(array, ("expert", "hsplit"), route)


def first_hop(array, k):
    return exchanged(array, INNER * k, k)


def second_hop(array, k):
    return exchanged(array, k, INNER * k)


def other_core(array):
    return lax.ppermute(array, "hsplit", [(0, 1), (1, 0)])


VMEM = pl.BlockSpec(memory_space=pltpu.VMEM)
HBM = pl.BlockSpec(memory_space=pltpu.HBM)
TILE = 256
WEIGHT = 3


def kept(rows, columns, dtype=jnp.bfloat16):
    return pltpu.VMEM((rows, columns), dtype)


def call(
    kernel, out_shape, args, name, flops=0, moved=0, specs=None, scratch=(), mib=4, aliases=None
):
    return pl.pallas_call(
        kernel,
        out_shape=out_shape,
        in_specs=specs or [VMEM] * len(args),
        out_specs=jax.tree.map(lambda _: VMEM, out_shape),
        scratch_shapes=scratch,
        input_output_aliases=aliases or {},
        compiler_params=pltpu.CompilerParams(vmem_limit_bytes=mib << 20),
        cost_estimate=pl.CostEstimate(
            flops=WEIGHT * flops, bytes_accessed=WEIGHT * moved, transcendentals=0
        ),
        name=name,
    )(*args)


def fetches(wanted):
    args = [pltpu.with_memory_space_constraint(w[0], pltpu.HBM) for w in wanted]
    specs = [HBM] * len(wanted)
    outs = []
    for weight, axis, _, _, span in wanted:
        shape = list(weight.shape)
        shape[axis] = span
        outs.append(kept(*shape))

    def copies(in_refs, out_refs, sems):
        found = []
        for n, (weight, axis, own, start, span) in enumerate(wanted):
            core = lax.axis_index("hsplit")
            core_at = core if own else 1 - core
            at = pl.multiple_of(core_at * (weight.shape[axis] // 2) + start, LANES)
            ref = in_refs[n]
            part = ref.at[:, pl.ds(at, span)] if axis else ref.at[pl.ds(at, span)]
            found.append(pltpu.make_async_copy(part, out_refs[n], sems.at[n]))
        return found

    scratch = [pltpu.SemaphoreType.DMA((len(wanted),))] if wanted else []
    moved = sum(2 * 2 * o.shape[0] * o.shape[1] for o in outs)
    return args, specs, outs, scratch, moved, copies


def fetch(wanted, name):
    args, specs, outs, scratch, moved, copies = fetches(wanted)

    def kernel(*refs):
        found = copies(refs[: len(args)], refs[len(args) : -2], refs[-1])
        for copy in found:
            copy.start()
        refs[-2][...] = jnp.zeros(refs[-2].shape, refs[-2].dtype)
        for copy in found:
            copy.wait()

    results = call(
        kernel, outs + [kept(8, LANES, jnp.float32)], args, name, moved=moved,
        specs=specs, scratch=scratch, mib=2,
    )
    return results[:-1], results[-1]


def beside(copies, compute):
    for copy in copies:
        copy.start()
    if copies:
        pl.when(lax.axis_index("hsplit") >= 0)(compute)
    else:
        compute()
    for copy in copies:
        copy.wait()


def tied(array, done, name):
    def kernel(*refs):
        del refs

    return call(kernel, kept(*array.shape), (array, *done), name, aliases={0: 0})


def first_piece(tokens, routes, route_weights):
    rows, width = tokens.shape
    half = width // 2

    def kernel(tok_in, routes_in, weights_in, out_ref, routes_ref, weights_ref, sems):
        at = pl.multiple_of(lax.axis_index("hsplit") * half, LANES)
        copies = [
            pltpu.make_async_copy(routes_in, routes_ref, sems.at[0]),
            pltpu.make_async_copy(weights_in, weights_ref, sems.at[1]),
            pltpu.make_async_copy(
                tok_in.at[:, pl.ds(at, half)], out_ref.at[:, pl.ds(0, half)], sems.at[2]
            ),
        ]
        for copy in copies:
            copy.start()
        copies[0].wait()
        copies[1].wait()
        expert = lax.broadcasted_iota(jnp.int32, (EXPERTS, rows), 0)
        table = jnp.zeros((EXPERTS, rows), jnp.float32)
        for k in range(routes_ref.shape[0]):
            named = routes_ref[k : k + 1, :] == expert
            table += jnp.where(named, weights_ref[k : k + 1, :], 0.0)
        high = table.astype(jnp.bfloat16)
        low = (table - high.astype(jnp.float32)).astype(jnp.bfloat16)
        both = jnp.concatenate([high, low], axis=0)
        shape = (2 * EXPERTS, LANES)
        lane = lax.broadcasted_iota(jnp.int32, shape, 1)
        place = (lax.broadcasted_iota(jnp.int32, shape, 0) == lane).astype(jnp.bfloat16)
        out_ref[:, half:] = lax.dot_general(
            both, place, (((0,), (0,)), ((), ())), preferred_element_type=jnp.float32
        ).astype(out_ref.dtype)
        copies[2].wait()

    args = (tokens, routes.T, route_weights.T)
    return call(
        kernel,
        kept(rows, half + LANES),
        [pltpu.with_memory_space_constraint(a, pltpu.HBM) for a in args],
        "first_piece",
        specs=[HBM] * 3,
        scratch=[
            pltpu.VMEM(args[1].shape, jnp.int32),
            pltpu.VMEM(args[2].shape, jnp.float32),
            pltpu.SemaphoreType.DMA((3,)),
        ],
    )


def joined(parts, done, name):
    rows, width = parts[0].shape

    def kernel(*refs):
        for k in range(len(parts)):
            refs[-1][k * rows : (k + 1) * rows] = refs[k][...]

    return call(kernel, kept(len(parts) * rows, width), (*parts, done), name)


def up_own(pieces, weights, wanted, before, name):
    units = weights[0].shape[1]
    depth = weights[0].shape[0]
    rows = sum(p.shape[0] for p in pieces)
    more, more_specs, fetched, scratch, moved, copies = fetches(wanted)
    fixed = list(pieces) + list(weights) + list(before)
    args = fixed + more
    shapes = [kept(rows, units, jnp.float32) for _ in range(2)]

    def kernel(*refs):
        outs = refs[len(args) : len(args) + 2]
        found = []
        if wanted:
            found = copies(refs[len(fixed) : len(args)], refs[len(args) + 2 : -1], refs[-1])

        def compute():
            for n in range(units // TILE):
                columns = slice(n * TILE, (n + 1) * TILE)
                x = jnp.concatenate([refs[p][:, :depth] for p in range(len(pieces))], axis=0)
                for which in range(2):
                    outs[which][:, columns] = jnp.dot(
                        x, refs[len(pieces) + which][:, columns], preferred_element_type=jnp.float32
                    )

        beside(found, compute)

    results = call(
        kernel, shapes + fetched, args, name, flops=4 * rows * units * depth, moved=moved,
        specs=[VMEM] * len(fixed) + more_specs, scratch=scratch,
    )
    return results[:2], results[2:]


def hidden_call(pieces, last, weights, own_sums, far_sums, extras, wanted):
    units = weights[0].shape[1]
    depth = weights[0].shape[0]
    rows = pieces[0].shape[0]
    block_rows = rows // INNER
    more, more_specs, fetched, scratch, moved, copies = fetches(wanted)
    fixed = list(pieces) + list(weights)
    sums_at = len(fixed)
    for _, gate, up in own_sums + far_sums:
        fixed += [gate, up]
    extras_at = len(fixed)
    fixed += list(extras)
    args = fixed + more
    out_shape = kept(INNER * rows, units)

    def kernel(*refs):
        out_ref = refs[len(args)]
        scale_ref = refs[-1]
        found = copies(refs[len(fixed) : len(args)], refs[len(args) + 1 : -2], refs[-2])
        def compute():
            extra = jnp.concatenate(
                [refs[extras_at + k][:, depth:] for k in range(INNER)], axis=0
            ).astype(jnp.float32)
            lane = lax.broadcasted_iota(jnp.int32, extra.shape, 1)
            expert = lax.axis_index("expert")
            mine = (lane == expert) | (lane == expert + EXPERTS)
            total = jnp.sum(jnp.where(mine, extra, 0.0), axis=1, keepdims=True)
            scale_ref[...] = jnp.broadcast_to(total, scale_ref.shape)

            for n in range(units // TILE):
                columns = slice(n * TILE, (n + 1) * TILE)
                x = jnp.concatenate([refs[p][:, :depth] for p in range(len(pieces))], axis=0)
                both = []
                for which in range(2):
                    product = jnp.dot(
                        x, refs[len(pieces) + which][:, columns], preferred_element_type=jnp.float32
                    )
                    own, far = {}, {}
                    for n_sum, (held, _, _) in enumerate(own_sums):
                        for at, k in enumerate(held):
                            own[k] = (refs[sums_at + 2 * n_sum + which], at)
                    for n_sum, (held, _, _) in enumerate(far_sums):
                        for at, k in enumerate(held):
                            far[k] = (refs[sums_at + 2 * (len(own_sums) + n_sum) + which], at)
                    parts = []
                    for jj in range(INNER):
                        for ii in range(INNER):
                            ref, at = own[jj]
                            at = at * rows + ii * block_rows
                            mine_part = ref[at : at + block_rows, columns]
                            if ii in far:
                                ref, at = far[ii]
                                at = at * rows + jj * block_rows
                                other = ref[at : at + block_rows, columns]
                            else:
                                at = last.index(ii) * rows + jj * block_rows
                                other = product[at : at + block_rows]
                            parts.append(mine_part + other)
                    both.append(jnp.concatenate(parts, axis=0))
                gate, up = both
                scale = jnp.concatenate([scale_ref[...]] * (TILE // LANES), axis=1)
                hidden = gate / (1.0 + jnp.exp(-gate)) * up * scale
                out_ref[:, columns] = hidden.astype(out_ref.dtype)

        beside(found, compute)

    results = call(
        kernel, [out_shape] + fetched, args, "hidden",
        flops=4 * len(pieces) * rows * units * depth, moved=moved,
        specs=[VMEM] * len(fixed) + more_specs,
        scratch=scratch + [pltpu.VMEM((INNER * rows, LANES), jnp.float32)],
    )
    return results[0], results[1:]


def down_far(hidden, weight, held, name, before=()):
    tokens, units = hidden.shape
    rows = tokens // INNER
    block_rows = rows // INNER
    span = weight.shape[1]

    def kernel(hid_ref, w_ref, *rest):
        out_ref = rest[-1]
        at = [jj * rows + k * block_rows for k in held for jj in range(INNER)]
        x = jnp.concatenate([hid_ref[a : a + block_rows] for a in at], axis=0)
        for at in range(0, span, TILE):
            out_ref[:, at : at + TILE] = jnp.dot(
                x, w_ref[:, at : at + TILE], preferred_element_type=jnp.float32
            ).astype(out_ref.dtype)

    out_rows = len(held) * rows
    return call(
        kernel, kept(out_rows, span), (hidden, weight, *before), name, flops=2 * out_rows * units * span
    )


def down_own(hidden, weight, received, held, name, before=()):
    tokens, units = hidden.shape
    rows = tokens // INNER
    span = weight.shape[1]

    def kernel(hid_ref, w_ref, far_ref, *rest):
        out_refs = rest[len(before) :]
        x = jnp.concatenate([hid_ref[k * rows : (k + 1) * rows] for k in held], axis=0)
        for at in range(0, span, TILE):
            columns = slice(at, at + TILE)
            total = jnp.dot(x, w_ref[:, columns], preferred_element_type=jnp.float32)
            total = (total + far_ref[:, columns].astype(jnp.float32)).astype(jnp.bfloat16)
            for n in range(len(held)):
                out_refs[n][:, columns] = total[n * rows : (n + 1) * rows]

    return call(
        kernel,
        [kept(rows, span) for _ in held],
        (hidden, weight, received, *before),
        name,
        flops=2 * len(held) * rows * units * span,
    )


def summed(refs):
    return functools.reduce(jnp.add, [ref[...].astype(jnp.float32) for ref in refs]).astype(
        jnp.bfloat16
    )


def add(*parts):
    def kernel(*refs):
        refs[-1][...] = summed(refs[:-1])

    return call(kernel, kept(*parts[0].shape), parts, "add")


def sum_split(parts, name):
    rows, span = parts[0].shape
    rows //= INNER

    def kernel(*refs):
        total = summed(refs[: len(parts)])
        for k in range(INNER):
            refs[len(parts) + k][...] = total[k * rows : (k + 1) * rows]

    return call(kernel, [kept(rows, span) for _ in range(INNER)], parts, name)


def sum_out(parts):
    def kernel(*refs):
        refs[INNER][...] = summed(refs[:INNER])

    return call(kernel, jax.ShapeDtypeStruct(parts[0].shape, jnp.bfloat16), parts, "sum_out")


def local_single(tokens, routes, route_weights, gate_weight, up_weight, down_weight):
    rows, width = tokens.shape
    half = width // 2
    gate_weight, up_weight, down_weight = gate_weight[0], up_weight[0], down_weight[0]
    first = first_piece(tokens, routes, route_weights)

    firsts = {0: first}
    for k in (3, 2, 1):
        firsts[k] = first_hop(first, k)
    (gate_mine,), done = fetch([(gate_weight, 0, True, 0, half)], "fetch_1")
    second = joined([firsts[k] for k in range(INNER)], done, "second")
    pieces = {0: second, 2: second_hop(second, 2), 1: second_hop(second, 1)}
    (up_mine, gate_other), done = fetch(
        [(up_weight, 0, True, 0, half), (gate_weight, 0, False, 0, half)], "fetch_2"
    )
    pieces[2] = tied(pieces[2], (pieces[1], done), "piece_2")
    pieces[3] = second_hop(pieces[2], 1)
    far = {k: other_core(pieces[k]) for k in (0, 2, 1)}

    early, late = (0, 2), (1, 3)
    own_early, (up_other,) = up_own(
        [pieces[k] for k in early], (gate_mine, up_mine), [(up_weight, 0, False, 0, half)], (),
        "up_own_early",
    )
    far_early, _ = up_own([far[k] for k in early], (gate_other, up_other), [], (), "up_far_early")
    pieces[3] = tied(pieces[3], far_early[:1], "piece_3")
    far[3] = other_core(pieces[3])
    own_late, (down_other,) = up_own(
        [pieces[k] for k in late], (gate_mine, up_mine), [(down_weight, 1, False, 0, half)],
        (), "up_own_late",
    )
    hidden, (down_mine,) = hidden_call(
        [far[k] for k in late],
        late,
        (gate_other, up_other),
        [(early, *own_early), (late, *own_late)],
        [(early, *far_early)],
        [pieces[k] for k in range(INNER)],
        [(down_weight, 1, True, 0, half)],
    )

    received, sums, before = {}, {}, ()
    halves = (((3, 1), "a"), ((2, 0), "b"))
    for held, name in halves:
        partial = down_far(hidden, down_other, held, "down_far_" + name, before)
        received[held] = other_core(partial)
        before = (partial,)
    before = ()
    for held, name in halves:
        parts = down_own(hidden, down_mine, received[held], held, "down_own_" + name, before)
        before = (parts[0],)
        sums.update(zip(held, parts))
    passed = add(sums[2], second_hop(sums[3], 1))
    split = sum_split([sums[0], second_hop(sums[1], 1), second_hop(passed, 2)], "sum_split")
    ended = [split[0]] + [first_hop(split[k], k) for k in (3, 2, 1)]
    return sum_out(ended)


def as_sent(array):

    def short(part):
        return part.astype(jnp.bfloat16) if part.dtype == jnp.float32 else part

    return jax.tree.map(short, array)


def swapped(block, axis, apart):
    count = lax.axis_size(axis)
    route = []
    for low in range(count):
        high = low | 1 << apart
        if high != low and high < count:
            route += [(low, high), (high, low)]
    return lax.ppermute(block, axis, route)


def expert_rows(tok_rows, full_gate, full_up, full_down):
    gate_value = jnp.dot(tok_rows, full_gate, preferred_element_type=jnp.float32)
    up_value = jnp.dot(tok_rows, full_up, preferred_element_type=jnp.float32)
    hidden = (jax.nn.silu(gate_value) * up_value).astype(jnp.bfloat16)
    partial_value = jnp.dot(hidden, full_down, preferred_element_type=jnp.float32)
    return lax.optimization_barrier(partial_value.astype(jnp.bfloat16))


def local_grouped(tokens, routes, route_weights, gate_weight, up_weight, down_weight):
    tok_dev, model_width = tokens.shape
    top_k = routes.shape[1]
    owners = lax.axis_size("expert")
    splits = lax.axis_size("hsplit")
    group_size = owners // EXPERTS
    group_bits = group_size.bit_length() - 1
    most = tok_dev // group_size
    slot_count = owners * most
    slice_width = model_width // group_size
    piece_width = slice_width // splits
    position = lax.axis_index("expert")
    token_group = lax.broadcasted_iota(jnp.int32, (tok_dev, top_k), 0) // most
    owner_of = (group_size * routes + token_group).reshape(-1)
    owner_hit = (owner_of[:, None] == jnp.arange(owners, dtype=jnp.int32)[None, :]).astype(
        jnp.int32
    )
    earlier = jnp.cumsum(owner_hit, axis=0) - owner_hit
    ranking = jnp.sum(earlier * owner_hit, axis=1)
    slot_of = owner_of * most + ranking
    slot_grid = slot_of.reshape(tok_dev, top_k)
    selector = jnp.any(
        slot_grid[:, :, None] == jnp.arange(slot_count, dtype=jnp.int32)[None, None, :], axis=1
    ).astype(jnp.bfloat16)
    outgoing = jnp.einsum("ts,td->sd", selector, tokens, preferred_element_type=jnp.float32).astype(
        jnp.bfloat16
    )
    outgoing = outgoing.reshape(owners, most, model_width)
    stacked = (gate_weight, up_weight, down_weight)
    for level in range(group_bits):
        partner = jax.tree.map(
            lambda part, own: part.astype(own.dtype),
            swapped(as_sent(stacked), "expert", level),
            stacked,
        )
        upper = position >> level & 1 == 1
        stacked = tuple(
            (
                jnp.where(
                    upper,
                    jnp.concatenate([far_piece, near_piece], axis=0),
                    jnp.concatenate([near_piece, far_piece], axis=0),
                )
                for near_piece, far_piece in zip(stacked, partner)
            )
        )
    share_units = gate_weight.shape[2]
    full_gate = stacked[0].reshape(model_width, share_units)
    full_up = stacked[1].reshape(model_width, share_units)
    full_down = stacked[2].transpose(1, 0, 2).reshape(share_units, group_size, splits, piece_width)
    full_down = full_down.transpose(0, 2, 1, 3).reshape(share_units, model_width)
    arrived = lax.all_to_all(outgoing, "expert", split_axis=0, concat_axis=0, tiled=True)
    flat_rows = arrived.reshape(-1, model_width)
    partials = expert_rows(flat_rows, full_gate, full_up, full_down).reshape(arrived.shape)
    partials = partials.reshape(slot_count, model_width)
    summed = lax.psum_scatter(
        partials.astype(jnp.float32).astype(jnp.bfloat16), "hsplit", scatter_dimension=1, tiled=True
    )
    results = summed.reshape(owners, most, -1)
    returned = lax.all_to_all(results, "expert", split_axis=0, concat_axis=0, tiled=True)
    picked = returned.reshape(slot_count, -1)[slot_of].astype(jnp.float32)
    weighted = picked.reshape(tok_dev, top_k, -1) * route_weights[:, :, None]
    return jnp.sum(weighted, axis=1).astype(jnp.bfloat16)


def solution(mesh):
    placed = (
        P("expert", None),
        P("expert", None),
        P("expert", None),
        P("expert", None, "hsplit"),
        P("expert", None, "hsplit"),
        P("expert", "hsplit", None),
    )
    single = mesh.shape["expert"] == EXPERTS and mesh.shape["hsplit"] == 2
    return jax.shard_map(
        local_single if single else local_grouped,
        mesh=mesh,
        in_specs=placed,
        out_specs=P("expert", "hsplit"),
        check_vma=False,
    )
```

```python
import functools

import jax
import jax.numpy as jnp
from jax import lax
from jax.experimental import pallas as pl
from jax.experimental.pallas import tpu as pltpu
from jax.sharding import PartitionSpec as P

EXPERTS = 16
LANES = 128
INNER = 4


def exchanged(array, even, odd):
    owners = lax.axis_size("expert")
    route = []
    for core, apart in enumerate((even, odd)):
        route += [(2 * i + core, 2 * (i ^ apart) + core) for i in range(owners)]
    return lax.ppermute(array, ("expert", "hsplit"), route)


def first_hop(array, k):
    return exchanged(array, INNER * k, k)


def second_hop(array, k):
    return exchanged(array, k, INNER * k)


def other_core(array):
    return lax.ppermute(array, "hsplit", [(0, 1), (1, 0)])


VMEM = pl.BlockSpec(memory_space=pltpu.VMEM)
HBM = pl.BlockSpec(memory_space=pltpu.HBM)
TILE = 256
WEIGHT = 3


def kept(rows, columns, dtype=jnp.bfloat16):
    return pltpu.VMEM((rows, columns), dtype)


def call(
    kernel, out_shape, args, name, flops=0, moved=0, specs=None, scratch=(), mib=4, aliases=None
):
    return pl.pallas_call(
        kernel,
        out_shape=out_shape,
        in_specs=specs or [VMEM] * len(args),
        out_specs=jax.tree.map(lambda _: VMEM, out_shape),
        scratch_shapes=scratch,
        input_output_aliases=aliases or {},
        compiler_params=pltpu.CompilerParams(vmem_limit_bytes=mib << 20),
        cost_estimate=pl.CostEstimate(
            flops=WEIGHT * flops, bytes_accessed=WEIGHT * moved, transcendentals=0
        ),
        name=name,
    )(*args)


def fetches(wanted):
    args = [pltpu.with_memory_space_constraint(w[0], pltpu.HBM) for w in wanted]
    specs = [HBM] * len(wanted)
    outs = []
    for weight, axis, _, _, span in wanted:
        shape = list(weight.shape)
        shape[axis] = span
        outs.append(kept(*shape))

    def copies(in_refs, out_refs, sems):
        found = []
        for n, (weight, axis, own, start, span) in enumerate(wanted):
            core = lax.axis_index("hsplit")
            core_at = core if own else 1 - core
            at = pl.multiple_of(core_at * (weight.shape[axis] // 2) + start, LANES)
            ref = in_refs[n]
            part = ref.at[:, pl.ds(at, span)] if axis else ref.at[pl.ds(at, span)]
            found.append(pltpu.make_async_copy(part, out_refs[n], sems.at[n]))
        return found

    scratch = [pltpu.SemaphoreType.DMA((len(wanted),))] if wanted else []
    moved = sum(2 * 2 * o.shape[0] * o.shape[1] for o in outs)
    return args, specs, outs, scratch, moved, copies


def fetch(wanted, name):
    args, specs, outs, scratch, moved, copies = fetches(wanted)

    def kernel(*refs):
        found = copies(refs[: len(args)], refs[len(args) : -2], refs[-1])
        for copy in found:
            copy.start()
        refs[-2][...] = jnp.zeros(refs[-2].shape, refs[-2].dtype)
        for copy in found:
            copy.wait()

    results = call(
        kernel, outs + [kept(8, LANES, jnp.float32)], args, name, moved=moved,
        specs=specs, scratch=scratch, mib=2,
    )
    return results[:-1], results[-1]


def beside(copies, compute):
    for copy in copies:
        copy.start()
    if copies:
        pl.when(lax.axis_index("hsplit") >= 0)(compute)
    else:
        compute()
    for copy in copies:
        copy.wait()


def tied(array, done, name):
    def kernel(*refs):
        del refs

    return call(kernel, kept(*array.shape), (array, *done), name, aliases={0: 0})


def first_piece(tokens, routes, route_weights):
    rows, width = tokens.shape
    half = width // 2

    def kernel(tok_in, routes_in, weights_in, out_ref, routes_ref, weights_ref, sems):
        at = pl.multiple_of(lax.axis_index("hsplit") * half, LANES)
        copies = [
            pltpu.make_async_copy(routes_in, routes_ref, sems.at[0]),
            pltpu.make_async_copy(weights_in, weights_ref, sems.at[1]),
            pltpu.make_async_copy(
                tok_in.at[:, pl.ds(at, half)], out_ref.at[:, pl.ds(0, half)], sems.at[2]
            ),
        ]
        for copy in copies:
            copy.start()
        copies[0].wait()
        copies[1].wait()
        expert = lax.broadcasted_iota(jnp.int32, (EXPERTS, rows), 0)
        table = jnp.zeros((EXPERTS, rows), jnp.float32)
        for k in range(routes_ref.shape[0]):
            named = routes_ref[k : k + 1, :] == expert
            table += jnp.where(named, weights_ref[k : k + 1, :], 0.0)
        high = table.astype(jnp.bfloat16)
        low = (table - high.astype(jnp.float32)).astype(jnp.bfloat16)
        both = jnp.concatenate([high, low], axis=0)
        shape = (2 * EXPERTS, LANES)
        lane = lax.broadcasted_iota(jnp.int32, shape, 1)
        place = (lax.broadcasted_iota(jnp.int32, shape, 0) == lane).astype(jnp.bfloat16)
        out_ref[:, half:] = lax.dot_general(
            both, place, (((0,), (0,)), ((), ())), preferred_element_type=jnp.float32
        ).astype(out_ref.dtype)
        copies[2].wait()

    args = (tokens, routes.T, route_weights.T)
    return call(
        kernel,
        kept(rows, half + LANES),
        [pltpu.with_memory_space_constraint(a, pltpu.HBM) for a in args],
        "first_piece",
        specs=[HBM] * 3,
        scratch=[
            pltpu.VMEM(args[1].shape, jnp.int32),
            pltpu.VMEM(args[2].shape, jnp.float32),
            pltpu.SemaphoreType.DMA((3,)),
        ],
    )


def joined(parts, done, name):
    rows, width = parts[0].shape

    def kernel(*refs):
        for k in range(len(parts)):
            refs[-1][k * rows : (k + 1) * rows] = refs[k][...]

    return call(kernel, kept(len(parts) * rows, width), (*parts, done), name)


def up_own(pieces, weights, wanted, before, name):
    units = weights[0].shape[1]
    depth = weights[0].shape[0]
    rows = sum(p.shape[0] for p in pieces)
    more, more_specs, fetched, scratch, moved, copies = fetches(wanted)
    fixed = list(pieces) + list(weights) + list(before)
    args = fixed + more
    shapes = [kept(rows, units, jnp.float32) for _ in range(2)]

    def kernel(*refs):
        outs = refs[len(args) : len(args) + 2]
        found = []
        if wanted:
            found = copies(refs[len(fixed) : len(args)], refs[len(args) + 2 : -1], refs[-1])

        def compute():
            for n in range(units // TILE):
                columns = slice(n * TILE, (n + 1) * TILE)
                x = jnp.concatenate([refs[p][:, :depth] for p in range(len(pieces))], axis=0)
                for which in range(2):
                    outs[which][:, columns] = jnp.dot(
                        x, refs[len(pieces) + which][:, columns], preferred_element_type=jnp.float32
                    )

        beside(found, compute)

    results = call(
        kernel, shapes + fetched, args, name, flops=4 * rows * units * depth, moved=moved,
        specs=[VMEM] * len(fixed) + more_specs, scratch=scratch,
    )
    return results[:2], results[2:]


def hidden_call(pieces, last, weights, own_sums, far_sums, extras, wanted):
    units = weights[0].shape[1]
    depth = weights[0].shape[0]
    rows = pieces[0].shape[0]
    block_rows = rows // INNER
    more, more_specs, fetched, scratch, moved, copies = fetches(wanted)
    fixed = list(pieces) + list(weights)
    sums_at = len(fixed)
    for _, gate, up in own_sums + far_sums:
        fixed += [gate, up]
    extras_at = len(fixed)
    fixed += list(extras)
    args = fixed + more
    out_shape = kept(INNER * rows, units)

    def kernel(*refs):
        out_ref = refs[len(args)]
        scale_ref = refs[-1]
        found = copies(refs[len(fixed) : len(args)], refs[len(args) + 1 : -2], refs[-2])
        def compute():
            extra = jnp.concatenate(
                [refs[extras_at + k][:, depth:] for k in range(INNER)], axis=0
            ).astype(jnp.float32)
            lane = lax.broadcasted_iota(jnp.int32, extra.shape, 1)
            expert = lax.axis_index("expert")
            mine = (lane == expert) | (lane == expert + EXPERTS)
            total = jnp.sum(jnp.where(mine, extra, 0.0), axis=1, keepdims=True)
            scale_ref[...] = jnp.broadcast_to(total, scale_ref.shape)

            for n in range(units // TILE):
                columns = slice(n * TILE, (n + 1) * TILE)
                x = jnp.concatenate([refs[p][:, :depth] for p in range(len(pieces))], axis=0)
                both = []
                for which in range(2):
                    product = jnp.dot(
                        x, refs[len(pieces) + which][:, columns], preferred_element_type=jnp.float32
                    )
                    own, far = {}, {}
                    for n_sum, (held, _, _) in enumerate(own_sums):
                        for at, k in enumerate(held):
                            own[k] = (refs[sums_at + 2 * n_sum + which], at)
                    for n_sum, (held, _, _) in enumerate(far_sums):
                        for at, k in enumerate(held):
                            far[k] = (refs[sums_at + 2 * (len(own_sums) + n_sum) + which], at)
                    parts = []
                    for jj in range(INNER):
                        for ii in range(INNER):
                            ref, at = own[jj]
                            at = at * rows + ii * block_rows
                            mine_part = ref[at : at + block_rows, columns]
                            if ii in far:
                                ref, at = far[ii]
                                at = at * rows + jj * block_rows
                                other = ref[at : at + block_rows, columns]
                            else:
                                at = last.index(ii) * rows + jj * block_rows
                                other = product[at : at + block_rows]
                            parts.append(mine_part + other)
                    both.append(jnp.concatenate(parts, axis=0))
                gate, up = both
                scale = jnp.concatenate([scale_ref[...]] * (TILE // LANES), axis=1)
                hidden = gate / (1.0 + jnp.exp(-gate)) * up * scale
                out_ref[:, columns] = hidden.astype(out_ref.dtype)

        beside(found, compute)

    results = call(
        kernel, [out_shape] + fetched, args, "hidden",
        flops=4 * len(pieces) * rows * units * depth, moved=moved,
        specs=[VMEM] * len(fixed) + more_specs,
        scratch=scratch + [pltpu.VMEM((INNER * rows, LANES), jnp.float32)],
    )
    return results[0], results[1:]


def product(x, weights, at):
    for weight in weights:
        if at < weight.shape[1]:
            return jnp.dot(x, weight[:, at : at + TILE], preferred_element_type=jnp.float32)
        at -= weight.shape[1]


def down_far(hidden, weight, held, name, before=()):
    tokens, units = hidden.shape
    rows = tokens // INNER
    block_rows = rows // INNER
    span = weight.shape[1]

    def kernel(hid_ref, w_ref, *rest):
        at = [jj * rows + k * block_rows for k in held for jj in range(INNER)]
        x = jnp.concatenate([hid_ref[a : a + block_rows] for a in at], axis=0)
        for at in range(0, span, TILE):
            total = product(x, [w_ref], at).astype(jnp.bfloat16)
            for n in range(len(held)):
                rest[len(before) + n][:, at : at + TILE] = total[n * rows : (n + 1) * rows]

    return call(
        kernel, [kept(rows, span) for _ in held], (hidden, weight, *before), name,
        flops=2 * len(held) * rows * units * span,
    )


def down_own(hidden, weights, received, held, name, before=()):
    tokens, units = hidden.shape
    rows = tokens // INNER
    span = sum(weight.shape[1] for weight in weights)
    args = (hidden, *weights, *received, *before)
    dtype = jnp.bfloat16 if received else jnp.float32

    def kernel(*refs):
        weight_refs = refs[1 : 1 + len(weights)]
        far_refs = refs[1 + len(weights) : 1 + len(weights) + len(received)]
        out_refs = refs[len(args) :]
        x = jnp.concatenate([refs[0][k * rows : (k + 1) * rows] for k in held], axis=0)
        for at in range(0, span, TILE):
            columns = slice(at, at + TILE)
            total = product(x, weight_refs, at)
            for n in range(len(held)):
                part = total[n * rows : (n + 1) * rows]
                if far_refs:
                    part = part + far_refs[n][:, columns].astype(jnp.float32)
                out_refs[n][:, columns] = part.astype(dtype)

    return call(
        kernel, [kept(rows, span, dtype) for _ in held], args, name,
        flops=2 * len(held) * rows * units * span,
    )


def summed(refs):
    return functools.reduce(jnp.add, [ref[...].astype(jnp.float32) for ref in refs]).astype(
        jnp.bfloat16
    )


def add(parts, name, cuts=None, before=()):
    rows, width = parts[0].shape
    cuts = cuts or [width]
    args = (*parts, *before)

    def kernel(*refs):
        at = 0
        for n, cut in enumerate(cuts):
            refs[len(args) + n][...] = summed([ref.at[:, pl.ds(at, cut)] for ref in refs[: len(parts)]])
            at += cut

    return call(kernel, [kept(rows, cut) for cut in cuts], args, name)


def add_side(whole, at, part, name):
    rows, width = part.shape

    def kernel(whole_ref, part_ref, out_ref):
        out_ref[...] = summed([whole_ref.at[:, pl.ds(at, width)], part_ref])

    return call(kernel, [kept(rows, width)], (whole, part), name)


def sum_split(parts, sides, name):
    rows, span = parts[0].shape
    rows //= INNER
    args = (*parts, *sides)

    def kernel(*refs):
        at = 0
        for n, side in enumerate(sides):
            width = side.shape[1]
            columns = pl.ds(at, width)
            total = summed([ref.at[:, columns] for ref in refs[: len(parts)]] + [refs[len(parts) + n]])
            for k in range(INNER):
                refs[len(args) + k][:, columns] = total[k * rows : (k + 1) * rows]
            at += width

    return call(kernel, [kept(rows, span) for _ in range(INNER)], args, name)


def sum_out(parts):
    def kernel(*refs):
        refs[INNER][...] = summed(refs[:INNER])

    return call(kernel, jax.ShapeDtypeStruct(parts[0].shape, jnp.bfloat16), parts, "sum_out")


def local_single(tokens, routes, route_weights, gate_weight, up_weight, down_weight):
    rows, width = tokens.shape
    half = width // 2
    gate_weight, up_weight, down_weight = gate_weight[0], up_weight[0], down_weight[0]
    first = first_piece(tokens, routes, route_weights)

    firsts = {0: first}
    for k in (3, 2, 1):
        firsts[k] = first_hop(first, k)
    (gate_mine,), done = fetch([(gate_weight, 0, True, 0, half)], "fetch_1")
    second = joined([firsts[k] for k in range(INNER)], done, "second")
    pieces = {0: second, 2: second_hop(second, 2), 1: second_hop(second, 1)}
    (up_mine, gate_other), done = fetch(
        [(up_weight, 0, True, 0, half), (gate_weight, 0, False, 0, half)], "fetch_2"
    )
    pieces[2] = tied(pieces[2], (pieces[1], done), "piece_2")
    pieces[3] = second_hop(pieces[2], 1)
    far = {k: other_core(pieces[k]) for k in (0, 2, 1)}

    early, late = (0, 2), (1, 3)
    own_early, (up_other,) = up_own(
        [pieces[k] for k in early], (gate_mine, up_mine), [(up_weight, 0, False, 0, half)], (),
        "up_own_early",
    )
    far_early, (down_other,) = up_own(
        [far[k] for k in early], (gate_other, up_other), [(down_weight, 1, False, 0, half)], (),
        "up_far_early",
    )
    pieces[3] = tied(pieces[3], far_early[:1], "piece_3")
    far[3] = other_core(pieces[3])
    side = half // 2
    own_late, (down_left,) = up_own(
        [pieces[k] for k in late], (gate_mine, up_mine), [(down_weight, 1, True, 0, side)],
        (), "up_own_late",
    )
    hidden, (down_right,) = hidden_call(
        [far[k] for k in late],
        late,
        (gate_other, up_other),
        [(early, *own_early), (late, *own_late)],
        [(early, *far_early)],
        [pieces[k] for k in range(INNER)],
        [(down_weight, 1, True, side, side)],
    )

    down_mine = (down_left, down_right)
    received, before = {}, ()
    for held, name in (((3, 1), "a"), ((2, 0), "b")):
        partial = down_far(hidden, down_other, held, "down_far_" + name, before)
        for k, part in zip(held, partial):
            received[k] = other_core(part)
        before = (partial[0],)
    mine_3, mine_1 = down_own(hidden, down_mine, (), (3, 1), "down_own_a", before)
    sides_3 = add((mine_3, received[3]), "sum_3", [side, half - side])
    passed = [second_hop(part, 1) for part in sides_3]
    (sum_1,) = add((mine_1, received[1]), "sum_1", before=sides_3)
    sum_2, sum_0 = down_own(hidden, down_mine, (received[2], received[0]), (2, 0), "down_own_b", (sum_1,))
    sum_1 = second_hop(sum_1, 1)
    sides_2, at = [], 0
    for n, part in enumerate(passed):
        (total,) = add_side(sum_2, at, part, "sum_2_%d" % n)
        sides_2.append(second_hop(total, 2))
        at += part.shape[1]
    split = sum_split([sum_0, sum_1], sides_2, "sum_split")
    ended = [split[0]] + [first_hop(split[k], k) for k in (3, 2, 1)]
    return sum_out(ended)


def as_sent(array):

    def short(part):
        return part.astype(jnp.bfloat16) if part.dtype == jnp.float32 else part

    return jax.tree.map(short, array)


def swapped(block, axis, apart):
    count = lax.axis_size(axis)
    route = []
    for low in range(count):
        high = low | 1 << apart
        if high != low and high < count:
            route += [(low, high), (high, low)]
    return lax.ppermute(block, axis, route)


def expert_rows(tok_rows, full_gate, full_up, full_down):
    gate_value = jnp.dot(tok_rows, full_gate, preferred_element_type=jnp.float32)
    up_value = jnp.dot(tok_rows, full_up, preferred_element_type=jnp.float32)
    hidden = (jax.nn.silu(gate_value) * up_value).astype(jnp.bfloat16)
    partial_value = jnp.dot(hidden, full_down, preferred_element_type=jnp.float32)
    return lax.optimization_barrier(partial_value.astype(jnp.bfloat16))


def local_grouped(tokens, routes, route_weights, gate_weight, up_weight, down_weight):
    tok_dev, model_width = tokens.shape
    top_k = routes.shape[1]
    owners = lax.axis_size("expert")
    splits = lax.axis_size("hsplit")
    group_size = owners // EXPERTS
    group_bits = group_size.bit_length() - 1
    most = tok_dev // group_size
    slot_count = owners * most
    slice_width = model_width // group_size
    piece_width = slice_width // splits
    position = lax.axis_index("expert")
    token_group = lax.broadcasted_iota(jnp.int32, (tok_dev, top_k), 0) // most
    owner_of = (group_size * routes + token_group).reshape(-1)
    owner_hit = (owner_of[:, None] == jnp.arange(owners, dtype=jnp.int32)[None, :]).astype(
        jnp.int32
    )
    earlier = jnp.cumsum(owner_hit, axis=0) - owner_hit
    ranking = jnp.sum(earlier * owner_hit, axis=1)
    slot_of = owner_of * most + ranking
    slot_grid = slot_of.reshape(tok_dev, top_k)
    selector = jnp.any(
        slot_grid[:, :, None] == jnp.arange(slot_count, dtype=jnp.int32)[None, None, :], axis=1
    ).astype(jnp.bfloat16)
    outgoing = jnp.einsum("ts,td->sd", selector, tokens, preferred_element_type=jnp.float32).astype(
        jnp.bfloat16
    )
    outgoing = outgoing.reshape(owners, most, model_width)
    stacked = (gate_weight, up_weight, down_weight)
    for level in range(group_bits):
        partner = jax.tree.map(
            lambda part, own: part.astype(own.dtype),
            swapped(as_sent(stacked), "expert", level),
            stacked,
        )
        upper = position >> level & 1 == 1
        stacked = tuple(
            (
                jnp.where(
                    upper,
                    jnp.concatenate([far_piece, near_piece], axis=0),
                    jnp.concatenate([near_piece, far_piece], axis=0),
                )
                for near_piece, far_piece in zip(stacked, partner)
            )
        )
    share_units = gate_weight.shape[2]
    full_gate = stacked[0].reshape(model_width, share_units)
    full_up = stacked[1].reshape(model_width, share_units)
    full_down = stacked[2].transpose(1, 0, 2).reshape(share_units, group_size, splits, piece_width)
    full_down = full_down.transpose(0, 2, 1, 3).reshape(share_units, model_width)
    arrived = lax.all_to_all(outgoing, "expert", split_axis=0, concat_axis=0, tiled=True)
    flat_rows = arrived.reshape(-1, model_width)
    partials = expert_rows(flat_rows, full_gate, full_up, full_down).reshape(arrived.shape)
    partials = partials.reshape(slot_count, model_width)
    summed = lax.psum_scatter(
        partials.astype(jnp.float32).astype(jnp.bfloat16), "hsplit", scatter_dimension=1, tiled=True
    )
    results = summed.reshape(owners, most, -1)
    returned = lax.all_to_all(results, "expert", split_axis=0, concat_axis=0, tiled=True)
    picked = returned.reshape(slot_count, -1)[slot_of].astype(jnp.float32)
    weighted = picked.reshape(tok_dev, top_k, -1) * route_weights[:, :, None]
    return jnp.sum(weighted, axis=1).astype(jnp.bfloat16)


def solution(mesh):
    placed = (
        P("expert", None),
        P("expert", None),
        P("expert", None),
        P("expert", None, "hsplit"),
        P("expert", None, "hsplit"),
        P("expert", "hsplit", None),
    )
    single = mesh.shape["expert"] == EXPERTS and mesh.shape["hsplit"] == 2
    return jax.shard_map(
        local_single if single else local_grouped,
        mesh=mesh,
        in_specs=placed,
        out_specs=P("expert", "hsplit"),
        check_vma=False,
    )
```

```python
import functools

import jax
import jax.numpy as jnp
from jax import lax
from jax.experimental import pallas as pl
from jax.experimental.pallas import tpu as pltpu
from jax.sharding import PartitionSpec as P

EXPERTS = 16
LANES = 128
INNER = 4


def exchanged(array, even, odd):
    owners = lax.axis_size("expert")
    route = []
    for core, apart in enumerate((even, odd)):
        route += [(2 * i + core, 2 * (i ^ apart) + core) for i in range(owners)]
    return lax.ppermute(array, ("expert", "hsplit"), route)


def first_hop(array, k):
    return exchanged(array, INNER * k, k)


def second_hop(array, k):
    return exchanged(array, k, INNER * k)


def other_core(array):
    return lax.ppermute(array, "hsplit", [(0, 1), (1, 0)])


VMEM = pl.BlockSpec(memory_space=pltpu.VMEM)
HBM = pl.BlockSpec(memory_space=pltpu.HBM)
TILE = 256
WEIGHT = 3


def kept(rows, columns, dtype=jnp.bfloat16):
    return pltpu.VMEM((rows, columns), dtype)


def call(
    kernel, out_shape, args, name, flops=0, moved=0, specs=None, scratch=(), mib=4, aliases=None
):
    return pl.pallas_call(
        kernel,
        out_shape=out_shape,
        in_specs=specs or [VMEM] * len(args),
        out_specs=jax.tree.map(lambda _: VMEM, out_shape),
        scratch_shapes=scratch,
        input_output_aliases=aliases or {},
        compiler_params=pltpu.CompilerParams(vmem_limit_bytes=mib << 20),
        cost_estimate=pl.CostEstimate(
            flops=WEIGHT * flops, bytes_accessed=WEIGHT * moved, transcendentals=0
        ),
        name=name,
    )(*args)


def fetches(wanted):
    args = [pltpu.with_memory_space_constraint(w[0], pltpu.HBM) for w in wanted]
    specs = [HBM] * len(wanted)
    outs = []
    for weight, axis, _, _, span, *columns in wanted:
        shape = list(weight.shape)
        shape[axis] = span
        if columns:
            shape[1] = columns[1]
        outs.append(kept(*shape))

    def copies(in_refs, out_refs, sems):
        found = []
        for n, (weight, axis, own, start, span, *columns) in enumerate(wanted):
            core = lax.axis_index("hsplit")
            core_at = core if own else 1 - core
            at = pl.multiple_of(core_at * (weight.shape[axis] // 2) + start, LANES)
            ref = in_refs[n]
            part = ref.at[:, pl.ds(at, span)] if axis else ref.at[pl.ds(at, span)]
            if columns:
                part = part.at[:, pl.ds(*columns)]
            found.append(pltpu.make_async_copy(part, out_refs[n], sems.at[n]))
        return found

    scratch = [pltpu.SemaphoreType.DMA((len(wanted),))] if wanted else []
    moved = sum(2 * 2 * o.shape[0] * o.shape[1] for o in outs)
    return args, specs, outs, scratch, moved, copies


def fetch(wanted, name):
    args, specs, outs, scratch, moved, copies = fetches(wanted)

    def kernel(*refs):
        found = copies(refs[: len(args)], refs[len(args) : -2], refs[-1])
        for copy in found:
            copy.start()
        refs[-2][...] = jnp.zeros(refs[-2].shape, refs[-2].dtype)
        for copy in found:
            copy.wait()

    results = call(
        kernel, outs + [kept(8, LANES, jnp.float32)], args, name, moved=moved,
        specs=specs, scratch=scratch, mib=2,
    )
    return results[:-1], results[-1]


def beside(copies, compute):
    for copy in copies:
        copy.start()
    if copies:
        pl.when(lax.axis_index("hsplit") >= 0)(compute)
    else:
        compute()
    for copy in copies:
        copy.wait()


def tied(array, done, name):
    def kernel(*refs):
        del refs

    return call(kernel, kept(*array.shape), (array, *done), name, aliases={0: 0})


def first_piece(tokens, routes, route_weights):
    rows, width = tokens.shape
    half = width // 2

    def kernel(tok_in, routes_in, weights_in, out_ref, routes_ref, weights_ref, sems):
        at = pl.multiple_of(lax.axis_index("hsplit") * half, LANES)
        copies = [
            pltpu.make_async_copy(routes_in, routes_ref, sems.at[0]),
            pltpu.make_async_copy(weights_in, weights_ref, sems.at[1]),
            pltpu.make_async_copy(
                tok_in.at[:, pl.ds(at, half)], out_ref.at[:, pl.ds(0, half)], sems.at[2]
            ),
        ]
        for copy in copies:
            copy.start()
        copies[0].wait()
        copies[1].wait()
        expert = lax.broadcasted_iota(jnp.int32, (EXPERTS, rows), 0)
        table = jnp.zeros((EXPERTS, rows), jnp.float32)
        for k in range(routes_ref.shape[0]):
            named = routes_ref[k : k + 1, :] == expert
            table += jnp.where(named, weights_ref[k : k + 1, :], 0.0)
        high = table.astype(jnp.bfloat16)
        low = (table - high.astype(jnp.float32)).astype(jnp.bfloat16)
        both = jnp.concatenate([high, low], axis=0)
        shape = (2 * EXPERTS, LANES)
        lane = lax.broadcasted_iota(jnp.int32, shape, 1)
        place = (lax.broadcasted_iota(jnp.int32, shape, 0) == lane).astype(jnp.bfloat16)
        out_ref[:, half:] = lax.dot_general(
            both, place, (((0,), (0,)), ((), ())), preferred_element_type=jnp.float32
        ).astype(out_ref.dtype)
        copies[2].wait()

    args = (tokens, routes.T, route_weights.T)
    return call(
        kernel,
        kept(rows, half + LANES),
        [pltpu.with_memory_space_constraint(a, pltpu.HBM) for a in args],
        "first_piece",
        specs=[HBM] * 3,
        scratch=[
            pltpu.VMEM(args[1].shape, jnp.int32),
            pltpu.VMEM(args[2].shape, jnp.float32),
            pltpu.SemaphoreType.DMA((3,)),
        ],
    )


def joined(parts, cut, done, name):
    rows, width = parts[0].shape
    total = len(parts) * rows

    def kernel(*refs):
        whole_ref, left_ref, right_ref = refs[-3:]
        for k in range(len(parts)):
            at = slice(k * rows, (k + 1) * rows)
            whole_ref[at] = refs[k][...]
            left_ref[at] = refs[k][:, :cut]
            right_ref[at] = refs[k][:, cut:]

    shapes = [kept(total, width), kept(total, cut), kept(total, width - cut)]
    return call(kernel, shapes, (*parts, done), name)


def flat(pieces):
    return [part for piece in pieces for part in piece]


def stacked(refs, pieces, depth):
    at, found = 0, []
    for piece in pieces:
        left, values = depth, []
        for part in piece:
            width = min(left, part.shape[1])
            values.append(refs[at][:, :width])
            left -= width
            at += 1
        found.append(jnp.concatenate(values, axis=1) if len(values) > 1 else values[0])
    return jnp.concatenate(found, axis=0)


def up_own(pieces, weights, wanted, before, name):
    units = sum(weight.shape[1] for weight in weights[0])
    depth = weights[0][0].shape[0]
    rows = sum(piece[0].shape[0] for piece in pieces)
    parts = flat(pieces)
    up_at = len(parts) + len(weights[0])
    weights_at = (slice(len(parts), up_at), slice(up_at, up_at + len(weights[1])))
    more, more_specs, fetched, scratch, moved, copies = fetches(wanted)
    fixed = parts + flat(weights) + list(before)
    args = fixed + more
    shapes = [kept(rows, units, jnp.float32) for _ in range(2)]

    def kernel(*refs):
        outs = refs[len(args) : len(args) + 2]
        found = []
        if wanted:
            found = copies(refs[len(fixed) : len(args)], refs[len(args) + 2 : -1], refs[-1])

        def compute():
            for n in range(units // TILE):
                columns = slice(n * TILE, (n + 1) * TILE)
                x = stacked(refs, pieces, depth)
                for which in range(2):
                    outs[which][:, columns] = product(x, refs[weights_at[which]], n * TILE)

        beside(found, compute)

    results = call(
        kernel, shapes + fetched, args, name, flops=4 * rows * units * depth, moved=moved,
        specs=[VMEM] * len(fixed) + more_specs, scratch=scratch,
    )
    return results[:2], results[2:]


def hidden_call(pieces, last, weights, own_sums, far_sums, extras, wanted):
    units = sum(weight.shape[1] for weight in weights[0])
    depth = weights[0][0].shape[0]
    rows = pieces[0][0].shape[0]
    parts = flat(pieces)
    up_at = len(parts) + len(weights[0])
    weights_at = (slice(len(parts), up_at), slice(up_at, up_at + len(weights[1])))
    block_rows = rows // INNER
    more, more_specs, fetched, scratch, moved, copies = fetches(wanted)
    fixed = parts + flat(weights)
    sums_at = len(fixed)
    for _, gate, up in own_sums + far_sums:
        fixed += [gate, up]
    extras_at = len(fixed)
    fixed += list(extras)
    args = fixed + more
    out_shape = kept(INNER * rows, units)

    def kernel(*refs):
        out_ref = refs[len(args)]
        scale_ref = refs[-1]
        found = copies(refs[len(fixed) : len(args)], refs[len(args) + 1 : -2], refs[-2])
        def compute():
            extra = jnp.concatenate(
                [refs[extras_at + k][:, -LANES:] for k in range(INNER)], axis=0
            ).astype(jnp.float32)
            lane = lax.broadcasted_iota(jnp.int32, extra.shape, 1)
            expert = lax.axis_index("expert")
            mine = (lane == expert) | (lane == expert + EXPERTS)
            total = jnp.sum(jnp.where(mine, extra, 0.0), axis=1, keepdims=True)
            scale_ref[...] = jnp.broadcast_to(total, scale_ref.shape)

            for n in range(units // TILE):
                columns = slice(n * TILE, (n + 1) * TILE)
                x = stacked(refs, pieces, depth)
                both = []
                for which in range(2):
                    last_sum = product(x, refs[weights_at[which]], n * TILE)
                    own, far = {}, {}
                    for n_sum, (held, _, _) in enumerate(own_sums):
                        for at, k in enumerate(held):
                            own[k] = (refs[sums_at + 2 * n_sum + which], at)
                    for n_sum, (held, _, _) in enumerate(far_sums):
                        for at, k in enumerate(held):
                            far[k] = (refs[sums_at + 2 * (len(own_sums) + n_sum) + which], at)
                    blocks = []
                    for jj in range(INNER):
                        for ii in range(INNER):
                            ref, at = own[jj]
                            at = at * rows + ii * block_rows
                            mine_part = ref[at : at + block_rows, columns]
                            if ii in far:
                                ref, at = far[ii]
                                at = at * rows + jj * block_rows
                                other = ref[at : at + block_rows, columns]
                            else:
                                at = last.index(ii) * rows + jj * block_rows
                                other = last_sum[at : at + block_rows]
                            blocks.append(mine_part + other)
                    both.append(jnp.concatenate(blocks, axis=0))
                gate, up = both
                scale = jnp.concatenate([scale_ref[...]] * (TILE // LANES), axis=1)
                hidden = gate / (1.0 + jnp.exp(-gate)) * up * scale
                out_ref[:, columns] = hidden.astype(out_ref.dtype)

        beside(found, compute)

    results = call(
        kernel, [out_shape] + fetched, args, "hidden",
        flops=4 * len(pieces) * rows * units * depth, moved=moved,
        specs=[VMEM] * len(fixed) + more_specs,
        scratch=scratch + [pltpu.VMEM((INNER * rows, LANES), jnp.float32)],
    )
    return results[0], results[1:]


def product(x, weights, at):
    for weight in weights:
        if at < weight.shape[1]:
            return jnp.dot(x, weight[:, at : at + TILE], preferred_element_type=jnp.float32)
        at -= weight.shape[1]


def down_far(hidden, weights, held, name, before=()):
    tokens, units = hidden.shape
    rows = tokens // INNER
    block_rows = rows // INNER
    span = sum(weight.shape[1] for weight in weights)

    def kernel(hid_ref, *rest):
        weight_refs, rest = rest[: len(weights)], rest[len(weights) :]
        at = [jj * rows + k * block_rows for k in held for jj in range(INNER)]
        x = jnp.concatenate([hid_ref[a : a + block_rows] for a in at], axis=0)
        for at in range(0, span, TILE):
            total = product(x, weight_refs, at).astype(jnp.bfloat16)
            for n in range(len(held)):
                rest[len(before) + n][:, at : at + TILE] = total[n * rows : (n + 1) * rows]

    return call(
        kernel, [kept(rows, span) for _ in held], (hidden, *weights, *before), name,
        flops=2 * len(held) * rows * units * span,
    )


def down_own(hidden, weights, received, held, name, before=()):
    tokens, units = hidden.shape
    rows = tokens // INNER
    span = sum(weight.shape[1] for weight in weights)
    args = (hidden, *weights, *received, *before)
    dtype = jnp.bfloat16 if received else jnp.float32

    def kernel(*refs):
        weight_refs = refs[1 : 1 + len(weights)]
        far_refs = refs[1 + len(weights) : 1 + len(weights) + len(received)]
        out_refs = refs[len(args) :]
        x = jnp.concatenate([refs[0][k * rows : (k + 1) * rows] for k in held], axis=0)
        for at in range(0, span, TILE):
            columns = slice(at, at + TILE)
            total = product(x, weight_refs, at)
            for n in range(len(held)):
                part = total[n * rows : (n + 1) * rows]
                if far_refs:
                    part = part + far_refs[n][:, columns].astype(jnp.float32)
                out_refs[n][:, columns] = part.astype(dtype)

    return call(
        kernel, [kept(rows, span, dtype) for _ in held], args, name,
        flops=2 * len(held) * rows * units * span,
    )


def summed(refs):
    return functools.reduce(jnp.add, [ref[...].astype(jnp.float32) for ref in refs]).astype(
        jnp.bfloat16
    )


def add(parts, name, cuts=None, before=()):
    rows, width = parts[0].shape
    cuts = cuts or [width]
    args = (*parts, *before)

    def kernel(*refs):
        at = 0
        for n, cut in enumerate(cuts):
            refs[len(args) + n][...] = summed([ref.at[:, pl.ds(at, cut)] for ref in refs[: len(parts)]])
            at += cut

    return call(kernel, [kept(rows, cut) for cut in cuts], args, name)


def add_side(whole, at, part, name):
    rows, width = part.shape

    def kernel(whole_ref, part_ref, out_ref):
        out_ref[...] = summed([whole_ref.at[:, pl.ds(at, width)], part_ref])

    return call(kernel, [kept(rows, width)], (whole, part), name)


def sum_split(parts, sides, name):
    rows, span = parts[0].shape
    rows //= INNER
    args = (*parts, *sides)

    def kernel(*refs):
        at = 0
        for n, side in enumerate(sides):
            width = side.shape[1]
            columns = pl.ds(at, width)
            total = summed([ref.at[:, columns] for ref in refs[: len(parts)]] + [refs[len(parts) + n]])
            for k in range(INNER):
                refs[len(args) + k][:, columns] = total[k * rows : (k + 1) * rows]
            at += width

    return call(kernel, [kept(rows, span) for _ in range(INNER)], args, name)


def sum_out(parts):
    def kernel(*refs):
        refs[INNER][...] = summed(refs[:INNER])

    return call(kernel, jax.ShapeDtypeStruct(parts[0].shape, jnp.bfloat16), parts, "sum_out")


def local_single(tokens, routes, route_weights, gate_weight, up_weight, down_weight):
    rows, width = tokens.shape
    half = width // 2
    gate_weight, up_weight, down_weight = gate_weight[0], up_weight[0], down_weight[0]
    first = first_piece(tokens, routes, route_weights)

    firsts = {0: first}
    for k in (3, 2, 1):
        firsts[k] = first_hop(first, k)
    side = half // 2
    (gate_mine, down_other_left), done = fetch(
        [(gate_weight, 0, True, 0, half), (down_weight, 1, False, 0, side)], "fetch_1"
    )
    second, left, right = joined([firsts[k] for k in range(INNER)], side, done, "second")
    pieces = {0: (second,), 2: [second_hop(left, 2), second_hop(right, 2)], 1: (second_hop(second, 1),)}
    first_units = up_weight.shape[1] // 2
    (up_mine, gate_other, up_other_left), done = fetch(
        [
            (up_weight, 0, True, 0, half),
            (gate_weight, 0, False, 0, half),
            (up_weight, 0, False, 0, half, 0, first_units),
        ],
        "fetch_2",
    )
    pieces[2][0] = tied(pieces[2][0], (*pieces[1], done), "piece_2")
    relays = [second_hop(part, 1) for part in pieces[2]]
    far = {k: [other_core(part) for part in pieces[k]] for k in (0, 2, 1)}
    early, late = (0, 2), (1, 3)
    mine = ((gate_mine,), (up_mine,))
    own_early, (up_other_right,) = up_own(
        [pieces[k] for k in early], mine,
        [(up_weight, 0, False, 0, half, first_units, first_units)], (), "up_own_early",
    )
    other = ((gate_other,), (up_other_left, up_other_right))
    far_early, (down_other_right,) = up_own(
        [far[k] for k in early], other, [(down_weight, 1, False, side, side)], (), "up_far_early"
    )
    down_other = (down_other_left, down_other_right)
    pieces[3] = [relays[0], tied(relays[1], far_early[:1], "piece_3")]
    far[3] = [other_core(part) for part in pieces[3]]
    own_late, (down_left,) = up_own(
        [pieces[k] for k in late], mine, [(down_weight, 1, True, 0, side)],
        (), "up_own_late",
    )
    hidden, (down_right,) = hidden_call(
        [far[k] for k in late],
        late,
        other,
        [(early, *own_early), (late, *own_late)],
        [(early, *far_early)],
        [pieces[k][-1] for k in range(INNER)],
        [(down_weight, 1, True, side, side)],
    )

    down_mine = (down_left, down_right)
    received, before = {}, ()
    for held, name in (((3, 1), "a"), ((2, 0), "b")):
        partial = down_far(hidden, down_other, held, "down_far_" + name, before)
        for k, part in zip(held, partial):
            received[k] = other_core(part)
        before = (partial[0],)
    mine_3, mine_1 = down_own(hidden, down_mine, (), (3, 1), "down_own_a", before)
    sides_3 = add((mine_3, received[3]), "sum_3", [side, half - side])
    passed = [second_hop(part, 1) for part in sides_3]
    (sum_1,) = add((mine_1, received[1]), "sum_1", before=sides_3)
    sum_2, sum_0 = down_own(hidden, down_mine, (received[2], received[0]), (2, 0), "down_own_b", (sum_1,))
    sum_1 = second_hop(sum_1, 1)
    sides_2, at = [], 0
    for n, part in enumerate(passed):
        (total,) = add_side(sum_2, at, part, "sum_2_%d" % n)
        sides_2.append(second_hop(total, 2))
        at += part.shape[1]
    split = sum_split([sum_0, sum_1], sides_2, "sum_split")
    ended = [split[0]] + [first_hop(split[k], k) for k in (3, 2, 1)]
    return sum_out(ended)


def as_sent(array):

    def short(part):
        return part.astype(jnp.bfloat16) if part.dtype == jnp.float32 else part

    return jax.tree.map(short, array)


def swapped(block, axis, apart):
    count = lax.axis_size(axis)
    route = []
    for low in range(count):
        high = low | 1 << apart
        if high != low and high < count:
            route += [(low, high), (high, low)]
    return lax.ppermute(block, axis, route)


def expert_rows(tok_rows, full_gate, full_up, full_down):
    gate_value = jnp.dot(tok_rows, full_gate, preferred_element_type=jnp.float32)
    up_value = jnp.dot(tok_rows, full_up, preferred_element_type=jnp.float32)
    hidden = (jax.nn.silu(gate_value) * up_value).astype(jnp.bfloat16)
    partial_value = jnp.dot(hidden, full_down, preferred_element_type=jnp.float32)
    return lax.optimization_barrier(partial_value.astype(jnp.bfloat16))


def local_grouped(tokens, routes, route_weights, gate_weight, up_weight, down_weight):
    tok_dev, model_width = tokens.shape
    top_k = routes.shape[1]
    owners = lax.axis_size("expert")
    splits = lax.axis_size("hsplit")
    group_size = owners // EXPERTS
    group_bits = group_size.bit_length() - 1
    most = tok_dev // group_size
    slot_count = owners * most
    slice_width = model_width // group_size
    piece_width = slice_width // splits
    position = lax.axis_index("expert")
    token_group = lax.broadcasted_iota(jnp.int32, (tok_dev, top_k), 0) // most
    owner_of = (group_size * routes + token_group).reshape(-1)
    owner_hit = (owner_of[:, None] == jnp.arange(owners, dtype=jnp.int32)[None, :]).astype(
        jnp.int32
    )
    earlier = jnp.cumsum(owner_hit, axis=0) - owner_hit
    ranking = jnp.sum(earlier * owner_hit, axis=1)
    slot_of = owner_of * most + ranking
    slot_grid = slot_of.reshape(tok_dev, top_k)
    selector = jnp.any(
        slot_grid[:, :, None] == jnp.arange(slot_count, dtype=jnp.int32)[None, None, :], axis=1
    ).astype(jnp.bfloat16)
    outgoing = jnp.einsum("ts,td->sd", selector, tokens, preferred_element_type=jnp.float32).astype(
        jnp.bfloat16
    )
    outgoing = outgoing.reshape(owners, most, model_width)
    stacked = (gate_weight, up_weight, down_weight)
    for level in range(group_bits):
        partner = jax.tree.map(
            lambda part, own: part.astype(own.dtype),
            swapped(as_sent(stacked), "expert", level),
            stacked,
        )
        upper = position >> level & 1 == 1
        stacked = tuple(
            (
                jnp.where(
                    upper,
                    jnp.concatenate([far_piece, near_piece], axis=0),
                    jnp.concatenate([near_piece, far_piece], axis=0),
                )
                for near_piece, far_piece in zip(stacked, partner)
            )
        )
    share_units = gate_weight.shape[2]
    full_gate = stacked[0].reshape(model_width, share_units)
    full_up = stacked[1].reshape(model_width, share_units)
    full_down = stacked[2].transpose(1, 0, 2).reshape(share_units, group_size, splits, piece_width)
    full_down = full_down.transpose(0, 2, 1, 3).reshape(share_units, model_width)
    arrived = lax.all_to_all(outgoing, "expert", split_axis=0, concat_axis=0, tiled=True)
    flat_rows = arrived.reshape(-1, model_width)
    partials = expert_rows(flat_rows, full_gate, full_up, full_down).reshape(arrived.shape)
    partials = partials.reshape(slot_count, model_width)
    summed = lax.psum_scatter(
        partials.astype(jnp.float32).astype(jnp.bfloat16), "hsplit", scatter_dimension=1, tiled=True
    )
    results = summed.reshape(owners, most, -1)
    returned = lax.all_to_all(results, "expert", split_axis=0, concat_axis=0, tiled=True)
    picked = returned.reshape(slot_count, -1)[slot_of].astype(jnp.float32)
    weighted = picked.reshape(tok_dev, top_k, -1) * route_weights[:, :, None]
    return jnp.sum(weighted, axis=1).astype(jnp.bfloat16)


def solution(mesh):
    placed = (
        P("expert", None),
        P("expert", None),
        P("expert", None),
        P("expert", None, "hsplit"),
        P("expert", None, "hsplit"),
        P("expert", "hsplit", None),
    )
    single = mesh.shape["expert"] == EXPERTS and mesh.shape["hsplit"] == 2
    return jax.shard_map(
        local_single if single else local_grouped,
        mesh=mesh,
        in_specs=placed,
        out_specs=P("expert", "hsplit"),
        check_vma=False,
    )
```

```python
import functools

import jax
import jax.numpy as jnp
from jax import lax
from jax.experimental import pallas as pl
from jax.experimental.pallas import tpu as pltpu
from jax.sharding import PartitionSpec as P

EXPERTS = 16
LANES = 128
INNER = 4


def exchanged(array, even, odd):
    owners = lax.axis_size("expert")
    route = []
    for core, apart in enumerate((even, odd)):
        route += [(2 * i + core, 2 * (i ^ apart) + core) for i in range(owners)]
    return lax.ppermute(array, ("expert", "hsplit"), route)


def first_hop(array, k):
    return exchanged(array, INNER * k, k)


def second_hop(array, k):
    return exchanged(array, k, INNER * k)


def other_core(array):
    return lax.ppermute(array, "hsplit", [(0, 1), (1, 0)])


VMEM = pl.BlockSpec(memory_space=pltpu.VMEM)
HBM = pl.BlockSpec(memory_space=pltpu.HBM)
TILE = 256
WEIGHT = 6


def kept(rows, columns, dtype=jnp.bfloat16):
    return pltpu.VMEM((rows, columns), dtype)


def call(
    kernel, out_shape, args, name, flops=0, moved=0, specs=None, scratch=(), mib=4, aliases=None
):
    return pl.pallas_call(
        kernel,
        out_shape=out_shape,
        in_specs=specs or [VMEM] * len(args),
        out_specs=jax.tree.map(lambda _: VMEM, out_shape),
        scratch_shapes=scratch,
        input_output_aliases=aliases or {},
        compiler_params=pltpu.CompilerParams(vmem_limit_bytes=mib << 20),
        cost_estimate=pl.CostEstimate(
            flops=WEIGHT * flops, bytes_accessed=WEIGHT * moved, transcendentals=0
        ),
        name=name,
    )(*args)


def fetches(wanted):
    args = [pltpu.with_memory_space_constraint(w[0], pltpu.HBM) for w in wanted]
    specs = [HBM] * len(wanted)
    outs = []
    for weight, axis, _, _, span, *columns in wanted:
        shape = list(weight.shape)
        shape[axis] = span
        if columns:
            shape[1] = columns[1]
        outs.append(kept(*shape))

    def copies(in_refs, out_refs, sems):
        found = []
        for n, (weight, axis, own, start, span, *columns) in enumerate(wanted):
            core = lax.axis_index("hsplit")
            core_at = core if own else 1 - core
            at = pl.multiple_of(core_at * (weight.shape[axis] // 2) + start, LANES)
            ref = in_refs[n]
            part = ref.at[:, pl.ds(at, span)] if axis else ref.at[pl.ds(at, span)]
            if columns:
                part = part.at[:, pl.ds(*columns)]
            found.append(pltpu.make_async_copy(part, out_refs[n], sems.at[n]))
        return found

    scratch = [pltpu.SemaphoreType.DMA((len(wanted),))] if wanted else []
    moved = sum(2 * 2 * o.shape[0] * o.shape[1] for o in outs)
    return args, specs, outs, scratch, moved, copies


def fetch(wanted, name):
    args, specs, outs, scratch, moved, copies = fetches(wanted)

    def kernel(*refs):
        found = copies(refs[: len(args)], refs[len(args) : -2], refs[-1])
        for copy in found:
            copy.start()
        refs[-2][...] = jnp.zeros(refs[-2].shape, refs[-2].dtype)
        for copy in found:
            copy.wait()

    results = call(
        kernel, outs + [kept(8, LANES, jnp.float32)], args, name, moved=moved,
        specs=specs, scratch=scratch, mib=2,
    )
    return results[:-1], results[-1]


def beside(copies, compute):
    for copy in copies:
        copy.start()
    if copies:
        pl.when(lax.axis_index("hsplit") >= 0)(compute)
    else:
        compute()
    for copy in copies:
        copy.wait()


def tied(array, done, name):
    def kernel(*refs):
        del refs

    return call(kernel, kept(*array.shape), (array, *done), name, aliases={0: 0})


def first_piece(tokens, routes, route_weights):
    rows, width = tokens.shape
    half = width // 2

    def kernel(tok_in, routes_in, weights_in, out_ref, routes_ref, weights_ref, sems):
        at = pl.multiple_of(lax.axis_index("hsplit") * half, LANES)
        copies = [
            pltpu.make_async_copy(routes_in, routes_ref, sems.at[0]),
            pltpu.make_async_copy(weights_in, weights_ref, sems.at[1]),
            pltpu.make_async_copy(
                tok_in.at[:, pl.ds(at, half)], out_ref.at[:, pl.ds(0, half)], sems.at[2]
            ),
        ]
        for copy in copies:
            copy.start()
        copies[0].wait()
        copies[1].wait()
        expert = lax.broadcasted_iota(jnp.int32, (EXPERTS, rows), 0)
        table = jnp.zeros((EXPERTS, rows), jnp.float32)
        for k in range(routes_ref.shape[0]):
            named = routes_ref[k : k + 1, :] == expert
            table += jnp.where(named, weights_ref[k : k + 1, :], 0.0)
        high = table.astype(jnp.bfloat16)
        low = (table - high.astype(jnp.float32)).astype(jnp.bfloat16)
        both = jnp.concatenate([high, low], axis=0)
        shape = (2 * EXPERTS, LANES)
        lane = lax.broadcasted_iota(jnp.int32, shape, 1)
        place = (lax.broadcasted_iota(jnp.int32, shape, 0) == lane).astype(jnp.bfloat16)
        out_ref[:, half:] = lax.dot_general(
            both, place, (((0,), (0,)), ((), ())), preferred_element_type=jnp.float32
        ).astype(out_ref.dtype)
        copies[2].wait()

    args = (tokens, routes.T, route_weights.T)
    return call(
        kernel,
        kept(rows, half + LANES),
        [pltpu.with_memory_space_constraint(a, pltpu.HBM) for a in args],
        "first_piece",
        specs=[HBM] * 3,
        scratch=[
            pltpu.VMEM(args[1].shape, jnp.int32),
            pltpu.VMEM(args[2].shape, jnp.float32),
            pltpu.SemaphoreType.DMA((3,)),
        ],
    )


def joined(parts, cut, done, name):
    rows, width = parts[0].shape
    total = len(parts) * rows

    def kernel(*refs):
        whole_ref, left_ref, right_ref = refs[-3:]
        for k in range(len(parts)):
            at = slice(k * rows, (k + 1) * rows)
            whole_ref[at] = refs[k][...]
            left_ref[at] = refs[k][:, :cut]
            right_ref[at] = refs[k][:, cut:]

    shapes = [kept(total, width), kept(total, cut), kept(total, width - cut)]
    return call(kernel, shapes, (*parts, done), name)


def flat(pieces):
    return [part for piece in pieces for part in piece]


def stacked(refs, pieces, depth):
    at, found = 0, []
    for piece in pieces:
        left, values = depth, []
        for part in piece:
            width = min(left, part.shape[1])
            values.append(refs[at][:, :width])
            left -= width
            at += 1
        found.append(jnp.concatenate(values, axis=1) if len(values) > 1 else values[0])
    return jnp.concatenate(found, axis=0)


def up_own(pieces, weights, wanted, before, name):
    units = sum(weight.shape[1] for weight in weights[0])
    depth = weights[0][0].shape[0]
    rows = sum(piece[0].shape[0] for piece in pieces)
    parts = flat(pieces)
    up_at = len(parts) + len(weights[0])
    weights_at = (slice(len(parts), up_at), slice(up_at, up_at + len(weights[1])))
    more, more_specs, fetched, scratch, moved, copies = fetches(wanted)
    fixed = parts + flat(weights) + list(before)
    args = fixed + more
    shapes = [kept(rows, units, jnp.float32) for _ in range(2)]

    def kernel(*refs):
        outs = refs[len(args) : len(args) + 2]
        found = []
        if wanted:
            found = copies(refs[len(fixed) : len(args)], refs[len(args) + 2 : -1], refs[-1])

        def compute():
            for n in range(units // TILE):
                columns = slice(n * TILE, (n + 1) * TILE)
                x = stacked(refs, pieces, depth)
                for which in range(2):
                    outs[which][:, columns] = product(x, refs[weights_at[which]], n * TILE)

        beside(found, compute)

    results = call(
        kernel, shapes + fetched, args, name, flops=4 * rows * units * depth, moved=moved,
        specs=[VMEM] * len(fixed) + more_specs, scratch=scratch,
    )
    return results[:2], results[2:]


def hidden_call(pieces, last, weights, own_sums, far_sums, extras, wanted):
    units = sum(weight.shape[1] for weight in weights[0])
    depth = weights[0][0].shape[0]
    rows = pieces[0][0].shape[0]
    parts = flat(pieces)
    up_at = len(parts) + len(weights[0])
    weights_at = (slice(len(parts), up_at), slice(up_at, up_at + len(weights[1])))
    block_rows = rows // INNER
    more, more_specs, fetched, scratch, moved, copies = fetches(wanted)
    fixed = parts + flat(weights)
    sums_at = len(fixed)
    for _, gate, up in own_sums + far_sums:
        fixed += [gate, up]
    extras_at = len(fixed)
    fixed += list(extras)
    args = fixed + more
    out_shape = kept(INNER * rows, units)

    def kernel(*refs):
        out_ref = refs[len(args)]
        scale_ref = refs[-1]
        found = copies(refs[len(fixed) : len(args)], refs[len(args) + 1 : -2], refs[-2])
        def compute():
            extra = jnp.concatenate(
                [refs[extras_at + k][:, -LANES:] for k in range(INNER)], axis=0
            ).astype(jnp.float32)
            lane = lax.broadcasted_iota(jnp.int32, extra.shape, 1)
            expert = lax.axis_index("expert")
            mine = (lane == expert) | (lane == expert + EXPERTS)
            total = jnp.sum(jnp.where(mine, extra, 0.0), axis=1, keepdims=True)
            scale_ref[...] = jnp.broadcast_to(total, scale_ref.shape)

            for n in range(units // TILE):
                columns = slice(n * TILE, (n + 1) * TILE)
                x = stacked(refs, pieces, depth)
                both = []
                for which in range(2):
                    last_sum = product(x, refs[weights_at[which]], n * TILE)
                    own, far = {}, {}
                    for n_sum, (held, _, _) in enumerate(own_sums):
                        for at, k in enumerate(held):
                            own[k] = (refs[sums_at + 2 * n_sum + which], at)
                    for n_sum, (held, _, _) in enumerate(far_sums):
                        for at, k in enumerate(held):
                            far[k] = (refs[sums_at + 2 * (len(own_sums) + n_sum) + which], at)
                    blocks = []
                    for jj in range(INNER):
                        for ii in range(INNER):
                            ref, at = own[jj]
                            at = at * rows + ii * block_rows
                            mine_part = ref[at : at + block_rows, columns]
                            if ii in far:
                                ref, at = far[ii]
                                at = at * rows + jj * block_rows
                                other = ref[at : at + block_rows, columns]
                            else:
                                at = last.index(ii) * rows + jj * block_rows
                                other = last_sum[at : at + block_rows]
                            blocks.append(mine_part + other)
                    both.append(jnp.concatenate(blocks, axis=0))
                gate, up = both
                scale = jnp.concatenate([scale_ref[...]] * (TILE // LANES), axis=1)
                hidden = gate / (1.0 + jnp.exp(-gate)) * up * scale
                out_ref[:, columns] = hidden.astype(out_ref.dtype)

        beside(found, compute)

    results = call(
        kernel, [out_shape] + fetched, args, "hidden",
        flops=4 * len(pieces) * rows * units * depth, moved=moved,
        specs=[VMEM] * len(fixed) + more_specs,
        scratch=scratch + [pltpu.VMEM((INNER * rows, LANES), jnp.float32)],
    )
    return results[0], results[1:]


def product(x, weights, at):
    for weight in weights:
        if at < weight.shape[1]:
            return jnp.dot(x, weight[:, at : at + TILE], preferred_element_type=jnp.float32)
        at -= weight.shape[1]


def down_far(hidden, weights, held, name, before=()):
    tokens, units = hidden.shape
    rows = tokens // INNER
    block_rows = rows // INNER
    span = sum(weight.shape[1] for weight in weights)

    def kernel(hid_ref, *rest):
        weight_refs, rest = rest[: len(weights)], rest[len(weights) :]
        at = [jj * rows + k * block_rows for k in held for jj in range(INNER)]
        x = jnp.concatenate([hid_ref[a : a + block_rows] for a in at], axis=0)
        for at in range(0, span, TILE):
            total = product(x, weight_refs, at).astype(jnp.bfloat16)
            for n in range(len(held)):
                rest[len(before) + n][:, at : at + TILE] = total[n * rows : (n + 1) * rows]

    return call(
        kernel, [kept(rows, span) for _ in held], (hidden, *weights, *before), name,
        flops=2 * len(held) * rows * units * span,
    )


def down_own(hidden, weights, received, held, name, before=()):
    tokens, units = hidden.shape
    rows = tokens // INNER
    span = sum(weight.shape[1] for weight in weights)
    args = (hidden, *weights, *received, *before)
    dtype = jnp.bfloat16 if received else jnp.float32

    def kernel(*refs):
        weight_refs = refs[1 : 1 + len(weights)]
        far_refs = refs[1 + len(weights) : 1 + len(weights) + len(received)]
        out_refs = refs[len(args) :]
        x = jnp.concatenate([refs[0][k * rows : (k + 1) * rows] for k in held], axis=0)
        for at in range(0, span, TILE):
            columns = slice(at, at + TILE)
            total = product(x, weight_refs, at)
            for n in range(len(held)):
                part = total[n * rows : (n + 1) * rows]
                if far_refs:
                    part = part + far_refs[n][:, columns].astype(jnp.float32)
                out_refs[n][:, columns] = part.astype(dtype)

    return call(
        kernel, [kept(rows, span, dtype) for _ in held], args, name,
        flops=2 * len(held) * rows * units * span,
    )


def summed(refs):
    return functools.reduce(jnp.add, [ref[...].astype(jnp.float32) for ref in refs]).astype(
        jnp.bfloat16
    )


def add(parts, name, cuts=None, before=()):
    rows, width = parts[0].shape
    cuts = cuts or [width]
    args = (*parts, *before)

    def kernel(*refs):
        at = 0
        for n, cut in enumerate(cuts):
            refs[len(args) + n][...] = summed([ref.at[:, pl.ds(at, cut)] for ref in refs[: len(parts)]])
            at += cut

    return call(kernel, [kept(rows, cut) for cut in cuts], args, name)


def add_side(whole, at, part, name):
    rows, width = part.shape

    def kernel(whole_ref, part_ref, out_ref):
        out_ref[...] = summed([whole_ref.at[:, pl.ds(at, width)], part_ref])

    return call(kernel, [kept(rows, width)], (whole, part), name)


def sum_split(parts, sides, name):
    rows, span = parts[0].shape
    rows //= INNER
    args = (*parts, *sides)

    def kernel(*refs):
        at = 0
        for n, side in enumerate(sides):
            width = side.shape[1]
            columns = pl.ds(at, width)
            total = summed([ref.at[:, columns] for ref in refs[: len(parts)]] + [refs[len(parts) + n]])
            for k in range(INNER):
                refs[len(args) + k][:, columns] = total[k * rows : (k + 1) * rows]
            at += width

    return call(kernel, [kept(rows, span) for _ in range(INNER)], args, name)


def sum_out(parts):
    def kernel(*refs):
        refs[INNER][...] = summed(refs[:INNER])

    return call(kernel, jax.ShapeDtypeStruct(parts[0].shape, jnp.bfloat16), parts, "sum_out")


def local_single(tokens, routes, route_weights, gate_weight, up_weight, down_weight):
    rows, width = tokens.shape
    half = width // 2
    gate_weight, up_weight, down_weight = gate_weight[0], up_weight[0], down_weight[0]
    first = first_piece(tokens, routes, route_weights)

    firsts = {0: first}
    for k in (3, 2, 1):
        firsts[k] = first_hop(first, k)
    side = half // 2
    first_units = up_weight.shape[1] // 2
    (gate_mine, down_other_left, up_other_left), done = fetch(
        [
            (gate_weight, 0, True, 0, half),
            (down_weight, 1, False, 0, side),
            (up_weight, 0, False, 0, half, 0, first_units),
        ],
        "fetch_1",
    )
    second, left, right = joined([firsts[k] for k in range(INNER)], side, done, "second")
    pieces = {0: (second,), 2: [second_hop(left, 2), second_hop(right, 2)], 1: (second_hop(second, 1),)}
    (up_mine, gate_other), done = fetch(
        [(up_weight, 0, True, 0, half), (gate_weight, 0, False, 0, half)], "fetch_2"
    )
    pieces[2][0] = tied(pieces[2][0], (*pieces[1], done), "piece_2")
    relays = [second_hop(part, 1) for part in pieces[2]]
    far = {k: [other_core(part) for part in pieces[k]] for k in (0, 2, 1)}
    early, late = (0, 2), (1, 3)
    mine = ((gate_mine,), (up_mine,))
    own_early, (up_other_right,) = up_own(
        [pieces[k] for k in early], mine,
        [(up_weight, 0, False, 0, half, first_units, first_units)], (), "up_own_early",
    )
    other = ((gate_other,), (up_other_left, up_other_right))
    far_early, (down_other_right,) = up_own(
        [far[k] for k in early], other, [(down_weight, 1, False, side, side)], (), "up_far_early"
    )
    down_other = (down_other_left, down_other_right)
    pieces[3] = [relays[0], tied(relays[1], far_early[:1], "piece_3")]
    far[3] = [other_core(part) for part in pieces[3]]
    own_late, (down_left,) = up_own(
        [pieces[k] for k in late], mine, [(down_weight, 1, True, 0, side)],
        (), "up_own_late",
    )
    hidden, (down_right,) = hidden_call(
        [far[k] for k in late],
        late,
        other,
        [(early, *own_early), (late, *own_late)],
        [(early, *far_early)],
        [pieces[k][-1] for k in range(INNER)],
        [(down_weight, 1, True, side, side)],
    )

    down_mine = (down_left, down_right)
    received, before = {}, ()
    for held, name in (((3, 1), "a"), ((2, 0), "b")):
        partial = down_far(hidden, down_other, held, "down_far_" + name, before)
        for k, part in zip(held, partial):
            received[k] = other_core(part)
        before = (partial[0],)
    mine_3, mine_1 = down_own(hidden, down_mine, (), (3, 1), "down_own_a", before)
    sides_3 = add((mine_3, received[3]), "sum_3", [side, half - side])
    passed = [second_hop(part, 1) for part in sides_3]
    (sum_1,) = add((mine_1, received[1]), "sum_1", before=sides_3)
    sum_2, sum_0 = down_own(hidden, down_mine, (received[2], received[0]), (2, 0), "down_own_b", (sum_1,))
    sum_1 = second_hop(sum_1, 1)
    sides_2, at = [], 0
    for n, part in enumerate(passed):
        (total,) = add_side(sum_2, at, part, "sum_2_%d" % n)
        sides_2.append(second_hop(total, 2))
        at += part.shape[1]
    split = sum_split([sum_0, sum_1], sides_2, "sum_split")
    ended = [split[0]] + [first_hop(split[k], k) for k in (3, 2, 1)]
    return sum_out(ended)


def as_sent(array):

    def short(part):
        return part.astype(jnp.bfloat16) if part.dtype == jnp.float32 else part

    return jax.tree.map(short, array)


def swapped(block, axis, apart):
    count = lax.axis_size(axis)
    route = []
    for low in range(count):
        high = low | 1 << apart
        if high != low and high < count:
            route += [(low, high), (high, low)]
    return lax.ppermute(block, axis, route)


def expert_rows(tok_rows, full_gate, full_up, full_down):
    gate_value = jnp.dot(tok_rows, full_gate, preferred_element_type=jnp.float32)
    up_value = jnp.dot(tok_rows, full_up, preferred_element_type=jnp.float32)
    hidden = (jax.nn.silu(gate_value) * up_value).astype(jnp.bfloat16)
    partial_value = jnp.dot(hidden, full_down, preferred_element_type=jnp.float32)
    return lax.optimization_barrier(partial_value.astype(jnp.bfloat16))


def local_grouped(tokens, routes, route_weights, gate_weight, up_weight, down_weight):
    tok_dev, model_width = tokens.shape
    top_k = routes.shape[1]
    owners = lax.axis_size("expert")
    splits = lax.axis_size("hsplit")
    group_size = owners // EXPERTS
    group_bits = group_size.bit_length() - 1
    most = tok_dev // group_size
    slot_count = owners * most
    slice_width = model_width // group_size
    piece_width = slice_width // splits
    position = lax.axis_index("expert")
    token_group = lax.broadcasted_iota(jnp.int32, (tok_dev, top_k), 0) // most
    owner_of = (group_size * routes + token_group).reshape(-1)
    owner_hit = (owner_of[:, None] == jnp.arange(owners, dtype=jnp.int32)[None, :]).astype(
        jnp.int32
    )
    earlier = jnp.cumsum(owner_hit, axis=0) - owner_hit
    ranking = jnp.sum(earlier * owner_hit, axis=1)
    slot_of = owner_of * most + ranking
    slot_grid = slot_of.reshape(tok_dev, top_k)
    selector = jnp.any(
        slot_grid[:, :, None] == jnp.arange(slot_count, dtype=jnp.int32)[None, None, :], axis=1
    ).astype(jnp.bfloat16)
    outgoing = jnp.einsum("ts,td->sd", selector, tokens, preferred_element_type=jnp.float32).astype(
        jnp.bfloat16
    )
    outgoing = outgoing.reshape(owners, most, model_width)
    stacked = (gate_weight, up_weight, down_weight)
    for level in range(group_bits):
        partner = jax.tree.map(
            lambda part, own: part.astype(own.dtype),
            swapped(as_sent(stacked), "expert", level),
            stacked,
        )
        upper = position >> level & 1 == 1
        stacked = tuple(
            (
                jnp.where(
                    upper,
                    jnp.concatenate([far_piece, near_piece], axis=0),
                    jnp.concatenate([near_piece, far_piece], axis=0),
                )
                for near_piece, far_piece in zip(stacked, partner)
            )
        )
    share_units = gate_weight.shape[2]
    full_gate = stacked[0].reshape(model_width, share_units)
    full_up = stacked[1].reshape(model_width, share_units)
    full_down = stacked[2].transpose(1, 0, 2).reshape(share_units, group_size, splits, piece_width)
    full_down = full_down.transpose(0, 2, 1, 3).reshape(share_units, model_width)
    arrived = lax.all_to_all(outgoing, "expert", split_axis=0, concat_axis=0, tiled=True)
    flat_rows = arrived.reshape(-1, model_width)
    partials = expert_rows(flat_rows, full_gate, full_up, full_down).reshape(arrived.shape)
    partials = partials.reshape(slot_count, model_width)
    summed = lax.psum_scatter(
        partials.astype(jnp.float32).astype(jnp.bfloat16), "hsplit", scatter_dimension=1, tiled=True
    )
    results = summed.reshape(owners, most, -1)
    returned = lax.all_to_all(results, "expert", split_axis=0, concat_axis=0, tiled=True)
    picked = returned.reshape(slot_count, -1)[slot_of].astype(jnp.float32)
    weighted = picked.reshape(tok_dev, top_k, -1) * route_weights[:, :, None]
    return jnp.sum(weighted, axis=1).astype(jnp.bfloat16)


def solution(mesh):
    placed = (
        P("expert", None),
        P("expert", None),
        P("expert", None),
        P("expert", None, "hsplit"),
        P("expert", None, "hsplit"),
        P("expert", "hsplit", None),
    )
    single = mesh.shape["expert"] == EXPERTS and mesh.shape["hsplit"] == 2
    return jax.shard_map(
        local_single if single else local_grouped,
        mesh=mesh,
        in_specs=placed,
        out_specs=P("expert", "hsplit"),
        check_vma=False,
    )
```

```python
import functools

import jax
import jax.numpy as jnp
from jax import lax
from jax.experimental import pallas as pl
from jax.experimental.pallas import tpu as pltpu
from jax.sharding import PartitionSpec as P

EXPERTS = 16
LANES = 128
INNER = 4


def exchanged(array, even, odd):
    owners = lax.axis_size("expert")
    route = []
    for core, apart in enumerate((even, odd)):
        route += [(2 * i + core, 2 * (i ^ apart) + core) for i in range(owners)]
    return lax.ppermute(array, ("expert", "hsplit"), route)


def first_hop(array, k):
    return exchanged(array, INNER * k, k)


def second_hop(array, k):
    return exchanged(array, k, INNER * k)


def other_core(array):
    return lax.ppermute(array, "hsplit", [(0, 1), (1, 0)])


VMEM = pl.BlockSpec(memory_space=pltpu.VMEM)
HBM = pl.BlockSpec(memory_space=pltpu.HBM)
TILE = 256
WEIGHT = 3


def kept(rows, columns, dtype=jnp.bfloat16):
    return pltpu.VMEM((rows, columns), dtype)


def call(
    kernel, out_shape, args, name, flops=0, moved=0, specs=None, scratch=(), mib=4, aliases=None
):
    return pl.pallas_call(
        kernel,
        out_shape=out_shape,
        in_specs=specs or [VMEM] * len(args),
        out_specs=jax.tree.map(lambda _: VMEM, out_shape),
        scratch_shapes=scratch,
        input_output_aliases=aliases or {},
        compiler_params=pltpu.CompilerParams(vmem_limit_bytes=mib << 20),
        cost_estimate=pl.CostEstimate(
            flops=WEIGHT * flops, bytes_accessed=WEIGHT * moved, transcendentals=0
        ),
        name=name,
    )(*args)


def fetches(wanted):
    args = [pltpu.with_memory_space_constraint(w[0], pltpu.HBM) for w in wanted]
    specs = [HBM] * len(wanted)
    outs = []
    for weight, axis, _, _, span, *columns in wanted:
        shape = list(weight.shape)
        shape[axis] = span
        if columns:
            shape[1] = columns[1]
        outs.append(kept(*shape))

    def copies(in_refs, out_refs, sems):
        found = []
        for n, (weight, axis, own, start, span, *columns) in enumerate(wanted):
            core = lax.axis_index("hsplit")
            core_at = core if own else 1 - core
            at = pl.multiple_of(core_at * (weight.shape[axis] // 2) + start, LANES)
            ref = in_refs[n]
            part = ref.at[:, pl.ds(at, span)] if axis else ref.at[pl.ds(at, span)]
            if columns:
                part = part.at[:, pl.ds(*columns)]
            found.append(pltpu.make_async_copy(part, out_refs[n], sems.at[n]))
        return found

    scratch = [pltpu.SemaphoreType.DMA((len(wanted),))] if wanted else []
    moved = sum(2 * 2 * o.shape[0] * o.shape[1] for o in outs)
    return args, specs, outs, scratch, moved, copies


def fetch(wanted, name):
    args, specs, outs, scratch, moved, copies = fetches(wanted)

    def kernel(*refs):
        found = copies(refs[: len(args)], refs[len(args) : -2], refs[-1])
        for copy in found:
            copy.start()
        refs[-2][...] = jnp.zeros(refs[-2].shape, refs[-2].dtype)
        for copy in found:
            copy.wait()

    results = call(
        kernel, outs + [kept(8, LANES, jnp.float32)], args, name, moved=moved,
        specs=specs, scratch=scratch, mib=2,
    )
    return results[:-1], results[-1]


def beside(copies, compute):
    for copy in copies:
        copy.start()
    if copies:
        pl.when(lax.axis_index("hsplit") >= 0)(compute)
    else:
        compute()
    for copy in copies:
        copy.wait()


def tied(array, done, name):
    def kernel(*refs):
        del refs

    return call(kernel, kept(*array.shape), (array, *done), name, aliases={0: 0})


def first_piece(tokens, routes, route_weights):
    rows, width = tokens.shape
    half = width // 2

    def kernel(tok_in, routes_in, weights_in, out_ref, routes_ref, weights_ref, sems):
        at = pl.multiple_of(lax.axis_index("hsplit") * half, LANES)
        copies = [
            pltpu.make_async_copy(routes_in, routes_ref, sems.at[0]),
            pltpu.make_async_copy(weights_in, weights_ref, sems.at[1]),
            pltpu.make_async_copy(
                tok_in.at[:, pl.ds(at, half)], out_ref.at[:, pl.ds(0, half)], sems.at[2]
            ),
        ]
        for copy in copies:
            copy.start()
        copies[0].wait()
        copies[1].wait()
        expert = lax.broadcasted_iota(jnp.int32, (EXPERTS, rows), 0)
        table = jnp.zeros((EXPERTS, rows), jnp.float32)
        for k in range(routes_ref.shape[0]):
            named = routes_ref[k : k + 1, :] == expert
            table += jnp.where(named, weights_ref[k : k + 1, :], 0.0)
        high = table.astype(jnp.bfloat16)
        low = (table - high.astype(jnp.float32)).astype(jnp.bfloat16)
        both = jnp.concatenate([high, low], axis=0)
        shape = (2 * EXPERTS, LANES)
        lane = lax.broadcasted_iota(jnp.int32, shape, 1)
        place = (lax.broadcasted_iota(jnp.int32, shape, 0) == lane).astype(jnp.bfloat16)
        out_ref[:, half:] = lax.dot_general(
            both, place, (((0,), (0,)), ((), ())), preferred_element_type=jnp.float32
        ).astype(out_ref.dtype)
        copies[2].wait()

    args = (tokens, routes.T, route_weights.T)
    return call(
        kernel,
        kept(rows, half + LANES),
        [pltpu.with_memory_space_constraint(a, pltpu.HBM) for a in args],
        "first_piece",
        specs=[HBM] * 3,
        scratch=[
            pltpu.VMEM(args[1].shape, jnp.int32),
            pltpu.VMEM(args[2].shape, jnp.float32),
            pltpu.SemaphoreType.DMA((3,)),
        ],
    )


def joined(parts, cut, done, name):
    rows, width = parts[0].shape
    total = len(parts) * rows

    def kernel(*refs):
        whole_ref, left_ref, right_ref = refs[-3:]
        for k in range(len(parts)):
            at = slice(k * rows, (k + 1) * rows)
            whole_ref[at] = refs[k][...]
            left_ref[at] = refs[k][:, :cut]
            right_ref[at] = refs[k][:, cut:]

    shapes = [kept(total, width), kept(total, cut), kept(total, width - cut)]
    return call(kernel, shapes, (*parts, done), name)


def flat(pieces):
    return [part for piece in pieces for part in piece]


def stacked(refs, pieces, depth):
    at, found = 0, []
    for piece in pieces:
        left, values = depth, []
        for part in piece:
            width = min(left, part.shape[1])
            values.append(refs[at][:, :width])
            left -= width
            at += 1
        found.append(jnp.concatenate(values, axis=1) if len(values) > 1 else values[0])
    return jnp.concatenate(found, axis=0)


def up_own(pieces, weights, wanted, before, name):
    units = sum(weight.shape[1] for weight in weights[0])
    depth = weights[0][0].shape[0]
    rows = sum(piece[0].shape[0] for piece in pieces)
    parts = flat(pieces)
    up_at = len(parts) + len(weights[0])
    weights_at = (slice(len(parts), up_at), slice(up_at, up_at + len(weights[1])))
    more, more_specs, fetched, scratch, moved, copies = fetches(wanted)
    fixed = parts + flat(weights) + list(before)
    args = fixed + more
    shapes = [kept(rows, units, jnp.float32) for _ in range(2)]

    def kernel(*refs):
        outs = refs[len(args) : len(args) + 2]
        found = []
        if wanted:
            found = copies(refs[len(fixed) : len(args)], refs[len(args) + 2 : -1], refs[-1])

        def compute():
            for n in range(units // TILE):
                columns = slice(n * TILE, (n + 1) * TILE)
                x = stacked(refs, pieces, depth)
                for which in range(2):
                    outs[which][:, columns] = product(x, refs[weights_at[which]], n * TILE)

        beside(found, compute)

    results = call(
        kernel, shapes + fetched, args, name, flops=4 * rows * units * depth, moved=moved,
        specs=[VMEM] * len(fixed) + more_specs, scratch=scratch,
    )
    return results[:2], results[2:]


def hidden_call(pieces, last, weights, own_sums, far_sums, extras, wanted):
    units = sum(weight.shape[1] for weight in weights[0])
    depth = weights[0][0].shape[0]
    rows = pieces[0][0].shape[0]
    parts = flat(pieces)
    up_at = len(parts) + len(weights[0])
    weights_at = (slice(len(parts), up_at), slice(up_at, up_at + len(weights[1])))
    block_rows = rows // INNER
    more, more_specs, fetched, scratch, moved, copies = fetches(wanted)
    fixed = parts + flat(weights)
    sums_at = len(fixed)
    for _, gate, up in own_sums + far_sums:
        fixed += [gate, up]
    extras_at = len(fixed)
    fixed += list(extras)
    args = fixed + more
    out_shape = kept(INNER * rows, units)

    def kernel(*refs):
        out_ref = refs[len(args)]
        scale_ref = refs[-1]
        found = copies(refs[len(fixed) : len(args)], refs[len(args) + 1 : -2], refs[-2])
        def compute():
            extra = jnp.concatenate(
                [refs[extras_at + k][:, -LANES:] for k in range(INNER)], axis=0
            ).astype(jnp.float32)
            lane = lax.broadcasted_iota(jnp.int32, extra.shape, 1)
            expert = lax.axis_index("expert")
            mine = (lane == expert) | (lane == expert + EXPERTS)
            total = jnp.sum(jnp.where(mine, extra, 0.0), axis=1, keepdims=True)
            scale_ref[...] = jnp.broadcast_to(total, scale_ref.shape)

            for n in range(units // TILE):
                columns = slice(n * TILE, (n + 1) * TILE)
                x = stacked(refs, pieces, depth)
                both = []
                for which in range(2):
                    last_sum = product(x, refs[weights_at[which]], n * TILE)
                    own, far = {}, {}
                    for n_sum, (held, _, _) in enumerate(own_sums):
                        for at, k in enumerate(held):
                            own[k] = (refs[sums_at + 2 * n_sum + which], at)
                    for n_sum, (held, _, _) in enumerate(far_sums):
                        for at, k in enumerate(held):
                            far[k] = (refs[sums_at + 2 * (len(own_sums) + n_sum) + which], at)
                    blocks = []
                    for jj in range(INNER):
                        for ii in range(INNER):
                            ref, at = own[jj]
                            at = at * rows + ii * block_rows
                            mine_part = ref[at : at + block_rows, columns]
                            if ii in far:
                                ref, at = far[ii]
                                at = at * rows + jj * block_rows
                                other = ref[at : at + block_rows, columns]
                            else:
                                at = last.index(ii) * rows + jj * block_rows
                                other = last_sum[at : at + block_rows]
                            blocks.append(mine_part + other)
                    both.append(jnp.concatenate(blocks, axis=0))
                gate, up = both
                scale = jnp.concatenate([scale_ref[...]] * (TILE // LANES), axis=1)
                hidden = gate / (1.0 + jnp.exp(-gate)) * up * scale
                out_ref[:, columns] = hidden.astype(out_ref.dtype)

        beside(found, compute)

    results = call(
        kernel, [out_shape] + fetched, args, "hidden",
        flops=4 * len(pieces) * rows * units * depth, moved=moved,
        specs=[VMEM] * len(fixed) + more_specs,
        scratch=scratch + [pltpu.VMEM((INNER * rows, LANES), jnp.float32)],
    )
    return results[0], results[1:]


def product(x, weights, at):
    for weight in weights:
        if at < weight.shape[1]:
            return jnp.dot(x, weight[:, at : at + TILE], preferred_element_type=jnp.float32)
        at -= weight.shape[1]


def down_far(hidden, weights, held, name, before=()):
    tokens, units = hidden.shape
    rows = tokens // INNER
    block_rows = rows // INNER
    span = sum(weight.shape[1] for weight in weights)

    def kernel(hid_ref, *rest):
        weight_refs, rest = rest[: len(weights)], rest[len(weights) :]
        at = [jj * rows + k * block_rows for k in held for jj in range(INNER)]
        x = jnp.concatenate([hid_ref[a : a + block_rows] for a in at], axis=0)
        for at in range(0, span, TILE):
            total = product(x, weight_refs, at).astype(jnp.bfloat16)
            for n in range(len(held)):
                rest[len(before) + n][:, at : at + TILE] = total[n * rows : (n + 1) * rows]

    return call(
        kernel, [kept(rows, span) for _ in held], (hidden, *weights, *before), name,
        flops=2 * len(held) * rows * units * span,
    )


def down_own(hidden, weights, received, held, name, before=()):
    tokens, units = hidden.shape
    rows = tokens // INNER
    span = sum(weight.shape[1] for weight in weights)
    args = (hidden, *weights, *received, *before)
    dtype = jnp.bfloat16 if received else jnp.float32

    def kernel(*refs):
        weight_refs = refs[1 : 1 + len(weights)]
        far_refs = refs[1 + len(weights) : 1 + len(weights) + len(received)]
        out_refs = refs[len(args) :]
        x = jnp.concatenate([refs[0][k * rows : (k + 1) * rows] for k in held], axis=0)
        for at in range(0, span, TILE):
            columns = slice(at, at + TILE)
            total = product(x, weight_refs, at)
            for n in range(len(held)):
                part = total[n * rows : (n + 1) * rows]
                if far_refs:
                    part = part + far_refs[n][:, columns].astype(jnp.float32)
                out_refs[n][:, columns] = part.astype(dtype)

    return call(
        kernel, [kept(rows, span, dtype) for _ in held], args, name,
        flops=2 * len(held) * rows * units * span,
    )


def summed(refs):
    return functools.reduce(jnp.add, [ref[...].astype(jnp.float32) for ref in refs]).astype(
        jnp.bfloat16
    )


def add(parts, name, cuts=None, before=()):
    rows, width = parts[0].shape
    cuts = cuts or [width]
    args = (*parts, *before)

    def kernel(*refs):
        at = 0
        for n, cut in enumerate(cuts):
            refs[len(args) + n][...] = summed([ref.at[:, pl.ds(at, cut)] for ref in refs[: len(parts)]])
            at += cut

    return call(kernel, [kept(rows, cut) for cut in cuts], args, name)


def add_side(whole, at, part, name):
    rows, width = part.shape

    def kernel(whole_ref, part_ref, out_ref):
        out_ref[...] = summed([whole_ref.at[:, pl.ds(at, width)], part_ref])

    return call(kernel, [kept(rows, width)], (whole, part), name)


def sum_split(parts, sides, name):
    rows, span = parts[0].shape
    rows //= INNER
    args = (*parts, *sides)

    def kernel(*refs):
        at = 0
        for n, side in enumerate(sides):
            width = side.shape[1]
            columns = pl.ds(at, width)
            total = summed([ref.at[:, columns] for ref in refs[: len(parts)]] + [refs[len(parts) + n]])
            for k in range(INNER):
                refs[len(args) + k][:, columns] = total[k * rows : (k + 1) * rows]
            at += width

    return call(kernel, [kept(rows, span) for _ in range(INNER)], args, name)


def sum_out(parts):
    def kernel(*refs):
        refs[INNER][...] = summed(refs[:INNER])

    return call(kernel, jax.ShapeDtypeStruct(parts[0].shape, jnp.bfloat16), parts, "sum_out")


def local_single(tokens, routes, route_weights, gate_weight, up_weight, down_weight):
    rows, width = tokens.shape
    half = width // 2
    gate_weight, up_weight, down_weight = gate_weight[0], up_weight[0], down_weight[0]
    first = first_piece(tokens, routes, route_weights)

    firsts = {0: first}
    for k in (3, 2, 1):
        firsts[k] = first_hop(first, k)
    side = half // 2
    first_units = up_weight.shape[1] // 2
    (gate_mine, down_other_left, up_other_left), done = fetch(
        [
            (gate_weight, 0, True, 0, half),
            (down_weight, 1, False, 0, side),
            (up_weight, 0, False, 0, half, 0, first_units),
        ],
        "fetch_1",
    )
    second, left, right = joined([firsts[k] for k in range(INNER)], side, done, "second")
    pieces = {0: (second,), 2: [second_hop(left, 2), second_hop(right, 2)], 1: (second_hop(second, 1),)}
    (up_mine, gate_other), done = fetch(
        [(up_weight, 0, True, 0, half), (gate_weight, 0, False, 0, half)], "fetch_2"
    )
    pieces[2][0] = tied(pieces[2][0], (*pieces[1], done), "piece_2")
    relays = [second_hop(part, 1) for part in pieces[2]]
    far = {k: [other_core(part) for part in pieces[k]] for k in (0, 2, 1)}
    early, late = (0, 2), (1, 3)
    mine = ((gate_mine,), (up_mine,))
    own_early, (up_other_right,) = up_own(
        [pieces[k] for k in early], mine,
        [(up_weight, 0, False, 0, half, first_units, first_units)], (), "up_own_early",
    )
    other = ((gate_other,), (up_other_left, up_other_right))
    far_early, (down_other_right,) = up_own(
        [far[k] for k in early], other, [(down_weight, 1, False, side, side)], (), "up_far_early"
    )
    down_other = (down_other_left, down_other_right)
    pieces[3] = [relays[0], tied(relays[1], far_early[:1], "piece_3")]
    far[3] = [other_core(part) for part in pieces[3]]
    own_late, (down_left,) = up_own(
        [pieces[k] for k in late], mine, [(down_weight, 1, True, 0, side)],
        (), "up_own_late",
    )
    hidden, (down_right,) = hidden_call(
        [far[k] for k in late],
        late,
        other,
        [(early, *own_early), (late, *own_late)],
        [(early, *far_early)],
        [pieces[k][-1] for k in range(INNER)],
        [(down_weight, 1, True, side, side)],
    )

    down_mine = (down_left, down_right)
    partial = {}
    partial[3], partial[1] = down_far(hidden, down_other, (3, 1), "down_far_a")
    partial[2], partial[0] = down_far(hidden, down_other, (2, 0), "down_far_b", (partial[3],))
    before = (partial[2],)
    received = {3: other_core(partial[3])}
    mine_3, mine_1 = down_own(hidden, down_mine, (), (3, 1), "down_own_a", before)
    sides_3 = add((mine_3, received[3]), "sum_3", [side, half - side])
    passed = [second_hop(part, 1) for part in sides_3]
    for k in (1, 2, 0):
        received[k] = other_core(tied(partial[k], sides_3, "far_%d" % k))
    (sum_1,) = add((mine_1, received[1]), "sum_1", before=sides_3)
    sum_2, sum_0 = down_own(hidden, down_mine, (received[2], received[0]), (2, 0), "down_own_b", (sum_1,))
    sum_1 = second_hop(sum_1, 1)
    sides_2, at = [], 0
    for n, part in enumerate(passed):
        (total,) = add_side(sum_2, at, part, "sum_2_%d" % n)
        sides_2.append(second_hop(total, 2))
        at += part.shape[1]
    split = sum_split([sum_0, sum_1], sides_2, "sum_split")
    ended = [split[0]] + [first_hop(split[k], k) for k in (3, 2, 1)]
    return sum_out(ended)


def as_sent(array):

    def short(part):
        return part.astype(jnp.bfloat16) if part.dtype == jnp.float32 else part

    return jax.tree.map(short, array)


def swapped(block, axis, apart):
    count = lax.axis_size(axis)
    route = []
    for low in range(count):
        high = low | 1 << apart
        if high != low and high < count:
            route += [(low, high), (high, low)]
    return lax.ppermute(block, axis, route)


def expert_rows(tok_rows, full_gate, full_up, full_down):
    gate_value = jnp.dot(tok_rows, full_gate, preferred_element_type=jnp.float32)
    up_value = jnp.dot(tok_rows, full_up, preferred_element_type=jnp.float32)
    hidden = (jax.nn.silu(gate_value) * up_value).astype(jnp.bfloat16)
    partial_value = jnp.dot(hidden, full_down, preferred_element_type=jnp.float32)
    return lax.optimization_barrier(partial_value.astype(jnp.bfloat16))


def local_grouped(tokens, routes, route_weights, gate_weight, up_weight, down_weight):
    tok_dev, model_width = tokens.shape
    top_k = routes.shape[1]
    owners = lax.axis_size("expert")
    splits = lax.axis_size("hsplit")
    group_size = owners // EXPERTS
    group_bits = group_size.bit_length() - 1
    most = tok_dev // group_size
    slot_count = owners * most
    slice_width = model_width // group_size
    piece_width = slice_width // splits
    position = lax.axis_index("expert")
    token_group = lax.broadcasted_iota(jnp.int32, (tok_dev, top_k), 0) // most
    owner_of = (group_size * routes + token_group).reshape(-1)
    owner_hit = (owner_of[:, None] == jnp.arange(owners, dtype=jnp.int32)[None, :]).astype(
        jnp.int32
    )
    earlier = jnp.cumsum(owner_hit, axis=0) - owner_hit
    ranking = jnp.sum(earlier * owner_hit, axis=1)
    slot_of = owner_of * most + ranking
    slot_grid = slot_of.reshape(tok_dev, top_k)
    selector = jnp.any(
        slot_grid[:, :, None] == jnp.arange(slot_count, dtype=jnp.int32)[None, None, :], axis=1
    ).astype(jnp.bfloat16)
    outgoing = jnp.einsum("ts,td->sd", selector, tokens, preferred_element_type=jnp.float32).astype(
        jnp.bfloat16
    )
    outgoing = outgoing.reshape(owners, most, model_width)
    stacked = (gate_weight, up_weight, down_weight)
    for level in range(group_bits):
        partner = jax.tree.map(
            lambda part, own: part.astype(own.dtype),
            swapped(as_sent(stacked), "expert", level),
            stacked,
        )
        upper = position >> level & 1 == 1
        stacked = tuple(
            (
                jnp.where(
                    upper,
                    jnp.concatenate([far_piece, near_piece], axis=0),
                    jnp.concatenate([near_piece, far_piece], axis=0),
                )
                for near_piece, far_piece in zip(stacked, partner)
            )
        )
    share_units = gate_weight.shape[2]
    full_gate = stacked[0].reshape(model_width, share_units)
    full_up = stacked[1].reshape(model_width, share_units)
    full_down = stacked[2].transpose(1, 0, 2).reshape(share_units, group_size, splits, piece_width)
    full_down = full_down.transpose(0, 2, 1, 3).reshape(share_units, model_width)
    arrived = lax.all_to_all(outgoing, "expert", split_axis=0, concat_axis=0, tiled=True)
    flat_rows = arrived.reshape(-1, model_width)
    partials = expert_rows(flat_rows, full_gate, full_up, full_down).reshape(arrived.shape)
    partials = partials.reshape(slot_count, model_width)
    summed = lax.psum_scatter(
        partials.astype(jnp.float32).astype(jnp.bfloat16), "hsplit", scatter_dimension=1, tiled=True
    )
    results = summed.reshape(owners, most, -1)
    returned = lax.all_to_all(results, "expert", split_axis=0, concat_axis=0, tiled=True)
    picked = returned.reshape(slot_count, -1)[slot_of].astype(jnp.float32)
    weighted = picked.reshape(tok_dev, top_k, -1) * route_weights[:, :, None]
    return jnp.sum(weighted, axis=1).astype(jnp.bfloat16)


def solution(mesh):
    placed = (
        P("expert", None),
        P("expert", None),
        P("expert", None),
        P("expert", None, "hsplit"),
        P("expert", None, "hsplit"),
        P("expert", "hsplit", None),
    )
    single = mesh.shape["expert"] == EXPERTS and mesh.shape["hsplit"] == 2
    return jax.shard_map(
        local_single if single else local_grouped,
        mesh=mesh,
        in_specs=placed,
        out_specs=P("expert", "hsplit"),
        check_vma=False,
    )
```
